128 devices in a mesh: row: 16 (over y, z), col: 8 (over x, core).
Axes of the slice: x: 4, y: 4, z: 4, core: 2. Of those that a mesh axis runs over, the one named last changes fastest.
Arguments:
- a_blocks: bfloat16 [2048, 8, 128, 128], P('row', 'col'), may hold values from -4 to 4
- p_tiles: bfloat16 [2048, 128, 128], P(('row', 'col')), may hold values from -0.5 to 0.5
- owner: int32 [2048, 1], P('row'), may hold values from 0 to 15; in each aligned block of 128 rows (0 to 127, 128 to 255, ...) at most 16 rows name the same one
- agg_local: int32 [2048], P('row'), may hold values from 0 to 1
- a_cols: int32 [2048, 8], P('row', 'col'), may hold values from 0 to 2047, as said below
Outputs:
- coarse: float32 [32, 32, 128, 128], P('row', 'col')
The draws below stay inside these ranges and needn't reach their ends.
Inputs may be any that keep to these rules, and one draw needn't show every extreme that they name: Column c of a_cols names a tile g with (g // 16) % 8 == c. Among the 128 tiles of one row slab at most 16 name the same owner, and in every draw some owner is named exactly 16 times by some slab.
All inputs are finite; a program needn't handle non-finite values.
Results may differ from the reference program's by a relative error of at most 0.0029.
Values may be sent and summed in bfloat16 or wider, within the bound.
A program may use at most 192 MiB of HBM per device.

```python
import math
import jax
import jax.numpy as jnp
import numpy as np
from jax import lax

B = 128
FTD = 16
OWN = 2
FTR = 128
TILES = 2048
CAP = 16
NAGG = 32
N_ROW = 16
N_COL = 8


def draw_a_cols(key, part):
    key = jax.random.fold_in(key, 7)
    first, second, third, fourth = jax.random.split(key, 4)
    home = (jnp.arange(TILES, dtype=jnp.int32) // FTR)[:, None]
    offset = jax.random.randint(fourth, (TILES, N_COL), -1, 2)
    near = jnp.clip(home + offset, 0, N_ROW - 1)
    far = jax.random.randint(first, (TILES, N_COL), 0, N_ROW)
    pick = jax.random.randint(third, (TILES, N_COL), 0, 8)
    slab = jnp.where(pick == 0, far, near)
    within = jax.random.randint(second, (TILES, N_COL), 0, FTD)
    column = jnp.arange(N_COL, dtype=jnp.int32)[None, :]
    return ((slab * N_COL + column) * FTD + within).astype(jnp.int32)


def touch_ends(array, key, least, largest):
    shape = array.shape
    index_at = [jax.random.randint(jax.random.fold_in(key, axis), (), 0, shape[axis]) for axis in range(len(shape))]
    array = array.at[tuple(index_at)].set(least)
    longest = shape.index(max(shape))
    index_at[longest] = (index_at[longest] + 1) % shape[longest]
    return array.at[tuple(index_at)].set(largest)


def level_of(key, dims, shards, low, high):
    def one(dim, shards_of):
        heights = jax.random.uniform(jax.random.fold_in(jax.random.fold_in(key, 6), dim), (shards_of,), jnp.float32, low / len(shards), high / len(shards))
        return jnp.repeat(jnp.exp(heights), dims[dim] // shards_of).reshape((-1,) + (1,) * (len(dims) - dim - 1))

    gain = one(*shards[0])
    for cut in shards[1:]:
        gain = gain * one(*cut)
    return gain


def shared_out(own_key, own, number, rows, number_of, top, most, lean):
    order = jax.random.permutation(own_key, number_of)
    crowded, usual = portions_of(number_of, rows * top, most, lean, True), portions_of(number_of, rows * top, most, lean, False)
    places = jnp.arange(number_of)

    def named(sizes, offset_by):
        used = int((sizes > 0).sum())
        fixed = max(1, used // 4)
        passed = fixed + (places - fixed + offset_by * (used - fixed)) % max(1, number_of - fixed)
        return jnp.zeros((number_of,), jnp.int32).at[order[jnp.where(places < fixed, places, passed)]].set(jnp.asarray(sizes, jnp.int32))

    sizes = jnp.where(number % 4 == 0, named(crowded, number // 4), named(usual, number - number // 4 - 1))
    mixed = jax.random.permutation(jax.random.fold_in(own, 3), number_of)
    source_of, receiver = mixed[0:number_of // 2 * 2:2], mixed[1:number_of // 2 * 2:2]
    margin = jnp.minimum(sizes[source_of] - 1, most - sizes[receiver]) // 2
    margin = jnp.where((source_of == order[0]) | (receiver == order[0]) | (sizes[receiver] == 0), 0, jnp.maximum(margin, 0))
    passed = jax.random.randint(jax.random.fold_in(own, 4), (number_of // 2,), 0, 1 << 20) % (margin + 1)
    sizes = sizes.at[source_of].add(-passed).at[receiver].add(passed)
    labels = jnp.searchsorted(jnp.cumsum(sizes), jnp.arange(rows * top), side="right").astype(jnp.int32)
    listing = labels.reshape(top, rows).T
    listing = listing[jax.random.permutation(jax.random.fold_in(own, 1), rows)]
    offset_by = jax.random.randint(jax.random.fold_in(own, 2), (rows, 1), 0, top)
    return jnp.take_along_axis(listing, (jnp.arange(top)[None, :] + offset_by) % top, axis=1)


def portions_of(count, total, most, slope, full):
    portions = [(1 << 20) // math.isqrt(grade ** slope) + 1 for grade in range(1, count + 1)]
    largest = most if full else min(most, max(-(-total // count), total * portions[0] // sum(portions)))
    least = 1 if total - largest >= count - 1 else 0
    holding, rest = [largest] + [least] * (count - 1), total - largest - least * (count - 1)
    while rest > 0:
        movable = [i for i in range(1, count) if holding[i] < largest] or [i for i in range(1, count) if holding[i] < most]
        mass, budget = sum([portions[i] for i in movable]), rest
        for i in movable:
            more = min(most - holding[i], max(1, budget * portions[i] // mass), rest)
            holding[i] = holding[i] + more
            rest = rest - more
    return np.array(holding)


def normal_values(stream_key, extent, spread, limit, cuts=(), kind=jnp.bfloat16):
    drawn = spread * jax.random.normal(stream_key, extent, jnp.float32)
    if cuts:
        drawn = drawn * level_of(stream_key, extent, cuts, -0.22, 0.18)
    return jnp.clip(drawn, -limit, limit).astype(kind)


def setup_inputs(seed: int = 0) -> dict:
    keys = jax.random.split(jax.random.key(seed), 6)
    a_blocks = normal_values(keys[0], (TILES, N_COL, B, B), 0.25, 4.0, ((0, 16), (1, 8)))
    p_tiles = normal_values(keys[1], (TILES, B, B), B ** -0.5, 0.5, ((0, 128),))
    owner_keys = jax.random.split(jax.random.fold_in(keys[2], 1), TILES // FTR)
    owner_turns = jax.random.permutation(jax.random.fold_in(keys[2], 3), TILES // FTR)
    owner = jax.vmap(lambda own, number: shared_out(jax.random.fold_in(keys[2], 2), own, number, FTR, N_ROW, 1, CAP, 1))(owner_keys, owner_turns).reshape((TILES, 1))
    agg_local = touch_ends(jax.random.randint(keys[3], (TILES,), 0, OWN), jax.random.fold_in(keys[3], 1), 0, OWN - 1).astype(jnp.int32)
    a_cols = draw_a_cols(jax.random.fold_in(keys[5], 71), 0)
    return {"a_blocks": a_blocks, "p_tiles": p_tiles, "owner": owner, "agg_local": agg_local, "a_cols": a_cols}


def reference(a_blocks, p_tiles, owner, agg_local, a_cols):
    aggregate = owner[:, 0] * OWN + agg_local
    groups = jnp.arange(TILES, dtype=jnp.int32).reshape(TILES // FTR, FTR)

    def accumulate(total, tiles):
        columns = a_cols[tiles]
        left = a_blocks[tiles].astype(jnp.float32)
        right = p_tiles[columns].astype(jnp.float32)
        product = jnp.einsum("tcij,tcjk->tcik", left, right).astype(jnp.bfloat16)
        row_side = p_tiles[tiles].astype(jnp.float32)
        contrib = jnp.einsum("tji,tcjk->tcik", row_side, product.astype(jnp.float32))
        where_to = aggregate[tiles][:, None] * NAGG + aggregate[columns]
        total = total.at[where_to.reshape(-1)].add(contrib.reshape(-1, B, B))
        return total, None

    start = jnp.zeros((NAGG * NAGG, B, B), jnp.float32)
    total, unused = lax.scan(accumulate, start, groups)
    return total.reshape(NAGG, NAGG, B, B)
```

```python
import functools

import jax
import jax.numpy as jnp
from jax import lax
from jax.experimental import pallas as pl
from jax.experimental.pallas import tpu as pltpu
from jax.sharding import PartitionSpec as P

MESH = pl.DeviceIdType.MESH
OWN = 2
B = 128
SIDE = 4
ROWS = 16
COLS = 8
TPD = 16
SLAB = 128
NAGG = 32
BLOCKS = NAGG * NAGG
GROUPS = 4
GT = SLAB // GROUPS
F32 = jnp.float32
BF16 = jnp.bfloat16


def iota(shape, dim):
    return lax.broadcasted_iota(jnp.int32, shape, dim)


def kernel(
    cols_ref, meta_ref, p_ref, a_hbm, out_ref,
    a_ref, panel, own, metas, hot, terms, sendbuf, recvbuf, xsend, xrecv, total, last,
    a_sem, loc_sem, meta_s, meta_r, ag_s, ag_r, x_s, x_r, ex_s, ex_r, cr_s, cr_r, fin_s, fin_r,
):
    row = lax.axis_index("row")
    col = lax.axis_index("col")
    y, z = row // SIDE, row % SIDE
    x, core = col // 2, col % 2

    def at(r, c):
        return {"row": r, "col": c}

    def remote(src, dst, ss, rs, dev):
        return pltpu.make_async_remote_copy(
            src_ref=src, dst_ref=dst, send_sem=ss, recv_sem=rs, device_id=dev, device_id_type=MESH
        )

    a_copy = pltpu.make_async_copy(a_hbm, a_ref, a_sem)
    a_copy.start()
    p_copy = pltpu.make_async_copy(p_ref, panel.at[row], loc_sem.at[0])
    p_copy.start()

    barrier = pltpu.get_barrier_semaphore()

    @pl.loop(1, ROWS)
    def _(d):
        pl.semaphore_signal(barrier, inc=1, device_id=at((row + d) % ROWS, col), device_id_type=MESH)

    @pl.loop(1, COLS)
    def _(d):
        pl.semaphore_signal(barrier, inc=1, device_id=at(row, (col + d) % COLS), device_id_type=MESH)

    pl.semaphore_wait(barrier, ROWS - 1 + COLS - 1)

    sends = []

    @pl.loop(1, ROWS)
    def _(d):
        remote(
            meta_ref, metas.at[row], meta_s.at[d], meta_r.at[d], at((row + d) % ROWS, col)
        ).start()

    counter = [0]

    class Half:
        def __init__(self, h):
            self.h = h
            self.f, self.s = (y, z) if h == 0 else (z, y)
            self.base = 8 * h
            self.sem = {}

        def slot(self, df, ds):
            f, s = (self.f + df) % SIDE, (self.s + ds) % SIDE
            return f * SIDE + s if self.h == 0 else s * SIDE + f

        def index(self, name):
            if name not in self.sem:
                self.sem[name] = counter[0]
                counter[0] += 1
            return self.sem[name]

        def send(self, name, slot, lo, n, to):
            k = self.index(name)
            src = p_ref.at[pl.ds(self.base + lo, n)] if slot == (0, 0) else panel.at[self.slot(*slot), pl.ds(self.base + lo, n)]
            c = remote(
                src, panel.at[self.slot(*slot), pl.ds(self.base + lo, n)],
                ag_s.at[k], ag_r.at[k], at(self.slot(*to), col),
            )
            c.start()
            sends.append(c)

        def recv(self, name, slot, lo, n):
            k = self.index(name)
            ref = panel.at[self.slot(*slot), pl.ds(self.base + lo, n)]
            remote(ref, ref, ag_s.at[k], ag_r.at[k], at(row, col)).wait_recv()

    halves = [Half(0), Half(1)]
    for h in halves:
        h.send("1+", (0, 0), 0, 8, (1, 0))
        h.send("1-", (0, 0), 0, 8, (-1, 0))
    for h in halves:
        h.send("2+0", (0, 0), 0, 8, (0, 1))
        h.send("2-0", (0, 0), 0, 8, (0, -1))

    for w in range(TPD):
        own[col, w] = p_ref[w].T
    right, left = (x + 1) % SIDE * 2 + core, (x + 3) % SIDE * 2 + core
    sib = x * 2 + 1 - core

    def xsend_to(k, c, lo, n, to):
        ref = own.at[c, pl.ds(lo, n)]
        cp = remote(ref, ref, x_s.at[k], x_r.at[k], at(row, to))
        cp.start()
        sends.append(cp)

    def xwait(k, c, lo, n):
        ref = own.at[c, pl.ds(lo, n)]
        remote(ref, ref, x_s.at[k], x_r.at[k], at(row, col)).wait_recv()

    far = (x + 2) % SIDE * 2 + core
    xsend_to(0, col, 0, TPD, right)
    xsend_to(1, col, 0, TPD, left)
    xsend_to(2, col, 0, TPD, sib)

    for h in halves:
        h.recv("1+", (-1, 0), 0, 8)
        h.send("1f+", (-1, 0), 0, 4, (1, 0))
        h.recv("1-", (1, 0), 0, 8)
        h.send("1f-", (1, 0), 4, 4, (-1, 0))
    for h in halves:
        for q in (-1, 1):
            h.send(f"2+{q}", (q, 0), 0, 8, (0, 1))
            h.send(f"2-{q}", (q, 0), 0, 8, (0, -1))

    def forward2(q):
        for h in halves:
            h.recv(f"2+{q}", (q, -1), 0, 8)
            h.send(f"2f+{q}", (q, -1), 0, 4, (0, 1))
            h.recv(f"2-{q}", (q, 1), 0, 8)
            h.send(f"2f-{q}", (q, 1), 4, 4, (0, -1))

    forward2(0)
    for h in halves:
        h.recv("1f+", (2, 0), 0, 4)
        h.recv("1f-", (2, 0), 4, 4)
        h.send("2+2", (2, 0), 0, 8, (0, 1))
        h.send("2-2", (2, 0), 0, 8, (0, -1))

    xwait(0, left, 0, TPD)
    xsend_to(3, left, 0, 8, right)
    xsend_to(5, left, 0, TPD, sib)
    xwait(1, right, 0, TPD)
    xsend_to(4, right, 8, 8, left)
    xsend_to(6, right, 0, TPD, sib)

    @pl.loop(1, ROWS)
    def _(d):
        ref = metas.at[(row + ROWS - d) % ROWS]
        remote(ref, ref, meta_s.at[d], meta_r.at[d], at(row, col)).wait_recv()

    metas[row] = meta_ref[...]
    aggs = jnp.concatenate([metas[r, 0:1, :] for r in range(ROWS)], 0).astype(F32).astype(BF16)
    for r in range(ROWS):
        g = metas[r, 1:2, :]
        lane_hot = jnp.where(iota((SLAB, SLAB), 0) == (g & (SLAB - 1)), 1.0, 0.0).astype(BF16)
        picked = jnp.dot(aggs, lane_hot, preferred_element_type=F32)
        slab_hot = iota((ROWS, SLAB), 0) == (g >> 7)
        big_j = jnp.sum(jnp.where(slab_hot, picked, 0.0), 0, keepdims=True).astype(jnp.int32)
        big_i = metas[r, 0:1, :]
        dest = (big_j >> 2) * SLAB + big_i * 4 + (big_j & 3)
        for blk in range(COLS):
            hot[blk * SLAB:(blk + 1) * SLAB, r * SLAB:(r + 1) * SLAB] = jnp.where(
                iota((SLAB, SLAB), 0) + blk * SLAB == dest, 1.0, 0.0
            ).astype(BF16)

    forward2(-1)
    forward2(1)

    xwait(3, far, 0, 8)
    xwait(4, far, 8, 8)
    xsend_to(7, far, 0, TPD, sib)

    forward2(2)
    for q in (0, -1, 1, 2):
        for h in halves:
            h.recv(f"2f+{q}", (q, 2), 0, 4)
            h.recv(f"2f-{q}", (q, 2), 4, 4)
    xwait(2, sib, 0, TPD)
    for k, cc in ((5, left), (6, right), (7, far)):
        xwait(k, cc + 1 - 2 * core, 0, TPD)
    p_copy.wait()
    a_copy.wait()

    for g in range(GROUPS):
        @pl.loop(0, GT // 4)
        def _(step):
            for u in range(4):
                t = g * GT + step * 4 + u
                tile = cols_ref[t]
                prod = jnp.dot(
                    a_ref[t, 0], panel[tile // SLAB, tile % TPD], preferred_element_type=F32
                ).astype(BF16)
                terms[pl.ds((step * 4 + u) * B, B), :] = jnp.dot(
                    own[t // TPD, t % TPD], prod, preferred_element_type=F32
                )

        @pl.loop(0, B // 8)
        def _(step):
            for u in range(8):
                i = step * 8 + u
                sendbuf[i, g * GT:(g + 1) * GT, :] = terms[pl.ds(i, GT, stride=B), :].astype(BF16)

        @pl.loop(1, ROWS)
        def _(d):
            to = (row + d) % ROWS
            remote(
                sendbuf.at[pl.ds(to * 8, 8), pl.ds(g * GT, GT)],
                recvbuf.at[row, :, pl.ds(g * GT, GT)],
                ex_s.at[g, d], ex_r.at[g, d], at(to, col),
            ).start()

    own_copy = pltpu.make_async_copy(sendbuf.at[pl.ds(row * 8, 8)], recvbuf.at[row], loc_sem.at[1])
    own_copy.start()
    own_copy.wait()
    for g in range(GROUPS):
        @pl.loop(1, ROWS)
        def _(d):
            ref = recvbuf.at[(row + ROWS - d) % ROWS, :, pl.ds(g * GT, GT)]
            remote(ref, ref, ex_s.at[g, d], ex_r.at[g, d], at(row, col)).wait_recv()

    @pl.loop(0, 4)
    def _(pair):
        rhs = jnp.concatenate(
            [recvbuf[:, pair * 2 + u].reshape(ROWS * SLAB, B) for u in range(2)], 1
        )

        @pl.loop(0, COLS)
        def _(blk):
            start = pl.multiple_of(blk * SLAB, SLAB)
            block = jnp.dot(hot[pl.ds(start, SLAB), :], rhs, preferred_element_type=F32)
            for u in range(2):
                xsend[blk, pair * 2 + u] = block[:, u * B:(u + 1) * B].astype(BF16)

        @pl.loop(1, COLS)
        def _(d):
            to = (col + d) % COLS
            remote(
                xsend.at[to, pl.ds(pair * 2, 2)], xrecv.at[col, pl.ds(pair * 2, 2)],
                cr_s.at[pair, d], cr_r.at[pair, d], at(row, to),
            ).start()

    total[...] = xsend[col].astype(F32)

    @pl.loop(1, COLS)
    def _(d):
        frm = (col + COLS - d) % COLS
        for pair in range(4):
            ref = xrecv.at[frm, pl.ds(pair * 2, 2)]
            remote(ref, ref, cr_s.at[pair, d], cr_r.at[pair, d], at(row, col)).wait_recv()
        total[...] += xrecv[frm].astype(F32)

    @pl.loop(1, ROWS)
    def _(d):
        to = (row + d) % ROWS
        remote(
            total.at[:, pl.ds(pl.multiple_of(to * 8, 8), 8)], last.at[pl.ds(row * 8, 8)],
            fin_s.at[d], fin_r.at[d], at(to, col),
        ).start()

    last[pl.ds(row * 8, 8)] = total[:, pl.ds(pl.multiple_of(row * 8, 8), 8), :]

    @pl.loop(1, ROWS)
    def _(d):
        ref = last.at[pl.ds((row + ROWS - d) % ROWS * 8, 8)]
        remote(ref, ref, fin_s.at[d], fin_r.at[d], at(row, col)).wait_recv()

    for b in range(8):
        out_ref[b // 4, b % 4] = last[:, b, :]

    for c in sends:
        c.wait_send()

    @pl.loop(1, ROWS)
    def _(d):
        to = (row + d) % ROWS
        remote(meta_ref, metas.at[row], meta_s.at[d], meta_r.at[d], at(to, col)).wait_send()
        for g in range(GROUPS):
            remote(
                sendbuf.at[pl.ds(to * 8, 8), pl.ds(g * GT, GT)],
                recvbuf.at[row, :, pl.ds(g * GT, GT)],
                ex_s.at[g, d], ex_r.at[g, d], at(to, col),
            ).wait_send()
        remote(
            total.at[:, pl.ds(pl.multiple_of(to * 8, 8), 8)], last.at[pl.ds(row * 8, 8)],
            fin_s.at[d], fin_r.at[d], at(to, col),
        ).wait_send()

    @pl.loop(1, COLS)
    def _(d):
        to = (col + d) % COLS
        for pair in range(4):
            remote(
                xsend.at[to, pl.ds(pair * 2, 2)], xrecv.at[col, pl.ds(pair * 2, 2)],
                cr_s.at[pair, d], cr_r.at[pair, d], at(row, to),
            ).wait_send()


def shards(a_blocks, p_tiles, owner, agg_local, a_cols):
    aggregate = owner[:, 0] * OWN + agg_local
    cols = a_cols[:, 0]
    meta = jnp.concatenate([aggregate[None], cols[None], jnp.zeros((6, SLAB), jnp.int32)], 0)
    vmem = pl.BlockSpec(memory_space=pltpu.VMEM)
    dma = pltpu.SemaphoreType.DMA
    return pl.pallas_call(
        kernel,
        out_shape=jax.ShapeDtypeStruct((OWN, 4, B, B), F32),
        in_specs=[
            pl.BlockSpec(memory_space=pltpu.SMEM), vmem, vmem, pl.BlockSpec(memory_space=pl.ANY)
        ],
        out_specs=vmem,
        scratch_shapes=[
            pltpu.VMEM((SLAB, 1, B, B), BF16),
            pltpu.VMEM((ROWS, TPD, B, B), BF16),
            pltpu.VMEM((COLS, TPD, B, B), BF16),
            pltpu.VMEM((ROWS, 8, SLAB), jnp.int32),
            pltpu.VMEM((BLOCKS, ROWS * SLAB), BF16),
            pltpu.VMEM((GT * B, B), F32),
            pltpu.VMEM((B, SLAB, B), BF16),
            pltpu.VMEM((ROWS, 8, SLAB, B), BF16),
            pltpu.VMEM((COLS, 8, SLAB, B), BF16),
            pltpu.VMEM((COLS, 8, SLAB, B), BF16),
            pltpu.VMEM((8, SLAB, B), F32),
            pltpu.VMEM((ROWS * 8, 8, B), F32),
            dma, dma((2,)), dma((ROWS,)), dma((ROWS,)),
            dma((40,)), dma((40,)), dma((8,)), dma((8,)),
            dma((GROUPS, ROWS)), dma((GROUPS, ROWS)), dma((4, COLS)), dma((4, COLS)),
            dma((ROWS,)), dma((ROWS,)),
        ],
        compiler_params=pltpu.CompilerParams(
            collective_id=0, has_side_effects=True, vmem_limit_bytes=56 * 1024 * 1024
        ),
    )(cols, meta, p_tiles, a_blocks)


def solution(mesh):
    in_specs = (
        P("row", "col", None, None),
        P(("row", "col"), None, None),
        P("row", None),
        P("row"),
        P("row", "col"),
    )
    out_specs = P("row", "col", None, None)
    return jax.shard_map(shards, mesh=mesh, in_specs=in_specs, out_specs=out_specs, check_vma=False)
```

```python
import functools

import jax
import jax.numpy as jnp
from jax import lax
from jax.experimental import pallas as pl
from jax.experimental.pallas import tpu as pltpu
from jax.sharding import PartitionSpec as P

MESH = pl.DeviceIdType.MESH
OWN = 2
B = 128
SIDE = 4
ROWS = 16
COLS = 8
TPD = 16
SLAB = 128
NAGG = 32
BLOCKS = NAGG * NAGG
GROUPS = 8
GT = SLAB // GROUPS
PARTS = (2, 2, 2, 1, 1)
CHUNKS = len(PARTS)
FROM = tuple(sum(PARTS[:n]) for n in range(CHUNKS))
UNROLL = 16
HOPS = (
    (1, 0), (3, 0), (0, 1), (0, 3), (1, 1), (3, 3), (1, 3), (3, 1),
    (2, 0), (0, 2), (2, 2), (1, 2), (2, 1), (3, 2), (2, 3),
)
F32 = jnp.float32
BF16 = jnp.bfloat16


def iota(shape, dim):
    return lax.broadcasted_iota(jnp.int32, shape, dim)


def kernel(
    cols_ref, owner_ref, local_ref, tiles_ref, p_ref, a_hbm, out_ref,
    a_ref, panel, own, metas, hot, terms, sendbuf, recvbuf, xsend, xrecv, total, last,
    a_sem, loc_sem, meta_s, meta_r, ag_s, ag_r, x_s, x_r, ex_s, ex_r, cr_s, cr_r, fin_s, fin_r,
):
    row = lax.axis_index("row")
    col = lax.axis_index("col")
    y, z = row >> 2, row & 3
    x, core = col >> 1, col & 1

    def at(r, c):
        return {"row": r, "col": c}

    def remote(src, dst, ss, rs, dev):
        return pltpu.make_async_remote_copy(
            src_ref=src, dst_ref=dst, send_sem=ss, recv_sem=rs, device_id=dev, device_id_type=MESH
        )

    def received(ref, ss, rs):
        remote(ref, ref, ss, rs, at(row, col)).wait_recv()

    def sent(ref, ss, rs):
        remote(ref, ref, ss, rs, at(row, col)).wait_send()

    right, left = ((x + 1) & 3) * 2 + core, ((x + 3) & 3) * 2 + core
    far = ((x + 2) & 3) * 2 + core
    sib = x * 2 + 1 - core

    barrier = pltpu.get_barrier_semaphore()
    near = [(((y + 1) & 3) * 4 + z, col), (((y + 3) & 3) * 4 + z, col), (y * 4 + ((z + 1) & 3), col),
            (y * 4 + ((z + 3) & 3), col), (row, right), (row, left), (row, sib)]
    for r, c in near:
        pl.semaphore_signal(barrier, inc=1, device_id=at(r, c), device_id_type=MESH)

    a_copy = pltpu.make_async_copy(a_hbm, a_ref, a_sem)
    a_copy.start()
    p_copy = pltpu.make_async_copy(p_ref, panel.at[pl.ds(row * TPD, TPD)], loc_sem.at[0])
    p_copy.start()
    metas[row] = jnp.concatenate(
        [owner_ref[...] * OWN + local_ref[...], tiles_ref[...], jnp.zeros((6, SLAB), jnp.int32)], 0
    )
    for w in range(TPD):
        own[col * TPD + w] = p_ref[w].T
    pl.semaphore_wait(barrier, len(near))

    class Half:
        sems = {}

        def __init__(self, h):
            self.h = h
            self.f, self.s = (y, z) if h == 0 else (z, y)

        def slot(self, df, ds):
            f, s = (self.f + df) & 3, (self.s + ds) & 3
            return f * SIDE + s if self.h == 0 else s * SIDE + f

        def sem(self, name):
            if name[:2] == "2f":
                return ag_r.at[0]
            return ag_r.at[Half.sems.setdefault((self.h, name), len(Half.sems) + 1)]

        def part(self, slot, lo, n):
            return panel.at[pl.ds(self.slot(*slot) * TPD + 8 * self.h + lo, n)]

        def send(self, name, slot, lo, n, to):
            src = p_ref.at[pl.ds(8 * self.h + lo, n)] if slot == (0, 0) else self.part(slot, lo, n)
            remote(src, self.part(slot, lo, n), ag_s, self.sem(name), at(self.slot(*to), col)).start()

        def recv(self, name, slot, lo, n):
            received(self.part(slot, lo, n), ag_s, self.sem(name))

    halves = [Half(0), Half(1)]
    for h in halves:
        h.send("1+", (0, 0), 0, 8, (1, 0))
        h.send("1-", (0, 0), 0, 8, (-1, 0))
    for h in halves:
        h.send("2+0", (0, 0), 0, 8, (0, 1))
        h.send("2-0", (0, 0), 0, 8, (0, -1))

    def own_send(k, c, lo, n, to):
        ref = own.at[pl.ds(c * TPD + lo, n)]
        remote(ref, ref, x_s, x_r.at[k], at(row, to)).start()

    def own_recv(k, c, lo, n):
        received(own.at[pl.ds(c * TPD + lo, n)], x_s, x_r.at[k])

    own_send(0, col, 0, TPD, right)
    own_send(1, col, 0, TPD, left)
    own_send(2, col, 0, TPD, sib)

    for h in halves:
        h.recv("1+", (-1, 0), 0, 8)
        h.send("1f+", (-1, 0), 0, 4, (1, 0))
        h.recv("1-", (1, 0), 0, 8)
        h.send("1f-", (1, 0), 4, 4, (-1, 0))
    for h in halves:
        for q in (-1, 1):
            h.send(f"2+{q}", (q, 0), 0, 8, (0, 1))
            h.send(f"2-{q}", (q, 0), 0, 8, (0, -1))

    def forward(q):
        for h in halves:
            h.recv(f"2+{q}", (q, -1), 0, 8)
            h.send("2f+", (q, -1), 0, 4, (0, 1))
            h.recv(f"2-{q}", (q, 1), 0, 8)
            h.send("2f-", (q, 1), 4, 4, (0, -1))

    forward(0)
    for h in halves:
        h.recv("1f+", (2, 0), 0, 4)
        h.recv("1f-", (2, 0), 4, 4)
        h.send("2+2", (2, 0), 0, 8, (0, 1))
        h.send("2-2", (2, 0), 0, 8, (0, -1))

    own_recv(0, left, 0, TPD)
    own_send(3, left, 0, 8, right)
    own_send(5, left, 0, TPD, sib)
    own_recv(1, right, 0, TPD)
    own_send(4, right, 8, 8, left)
    own_send(6, right, 0, TPD, sib)

    forward(-1)
    forward(1)
    own_recv(3, far, 0, 8)
    own_recv(4, far, 8, 8)
    own_send(7, far, 0, TPD, sib)
    forward(2)
    own_recv(2, sib, 0, TPD)
    for k, c in ((5, left), (6, right), (7, far)):
        own_recv(k, c + 1 - 2 * core, 0, TPD)
    p_copy.wait()
    a_copy.wait()
    received(panel.at[pl.ds(0, 64)], ag_s, ag_r.at[0])

    @pl.loop(1, ROWS)
    def _(d):
        remote(metas.at[row], metas.at[row], meta_s, meta_r, at((row + d) & 15, col)).start()

    def exchange(chunk, lo, n):
        for dy, dz in HOPS:
            to = ((y + dy) & 3) * 4 + ((z + dz) & 3)
            remote(
                sendbuf.at[pl.ds(to * 8 + FROM[chunk], PARTS[chunk]), pl.ds(lo, n)],
                recvbuf.at[pl.ds(FROM[chunk], PARTS[chunk]), row, pl.ds(lo, n)],
                ex_s, ex_r.at[chunk], at(to, col),
            ).start()

    for g in range(GROUPS):
        @pl.loop(0, GT // UNROLL)
        def _(step):
            for u in range(UNROLL):
                t = g * GT + step * UNROLL + u
                tile = cols_ref[t]
                prod = jnp.dot(
                    a_ref[t, 0], panel[(tile >> 7) * TPD + (tile & 15)], preferred_element_type=F32
                ).astype(BF16)
                terms[pl.ds((step * UNROLL + u) * B, B), :] = jnp.dot(
                    own[t], prod, preferred_element_type=F32
                )

        @pl.loop(0, B // 8)
        def _(step):
            for u in range(8):
                i = step * 8 + u
                sendbuf[i, g * GT:(g + 1) * GT, :] = terms[pl.ds(i, GT, stride=B), :].astype(BF16)

        exchange(0, g * GT, GT)

    own_copies = [
        pltpu.make_async_copy(sendbuf.at[row * 8 + i], recvbuf.at[i, row], loc_sem.at[1 + i])
        for i in range(8)
    ]
    for c in own_copies:
        c.start()
    exchange(1, 0, SLAB)

    received(metas.at[pl.ds(0, ROWS - 1)], meta_s, meta_r)
    aggs = jnp.concatenate([metas[r, 0:1, :] for r in range(ROWS)], 0).astype(F32).astype(BF16)
    for r in range(ROWS):
        g = metas[r, 1:2, :]
        lane_hot = jnp.where(iota((SLAB, SLAB), 0) == (g & (SLAB - 1)), 1.0, 0.0).astype(BF16)
        picked = jnp.dot(aggs, lane_hot, preferred_element_type=F32)
        slab_hot = iota((ROWS, SLAB), 0) == (g >> 7)
        big_j = jnp.sum(jnp.where(slab_hot, picked, 0.0), 0, keepdims=True).astype(jnp.int32)
        big_i = metas[r, 0:1, :]
        dest = (big_j >> 2) * SLAB + big_i * 4 + (big_j & 3)
        for blk in range(COLS):
            hot[blk * SLAB:(blk + 1) * SLAB, r * SLAB:(r + 1) * SLAB] = jnp.where(
                iota((SLAB, SLAB), 0) + blk * SLAB == dest, 1.0, 0.0
            ).astype(BF16)
    for c in own_copies:
        c.wait()

    def scatter(chunk):
        lo, n = FROM[chunk], PARTS[chunk]
        rhs = jnp.concatenate([recvbuf[lo + u].reshape(ROWS * SLAB, B) for u in range(n)], 1)

        @pl.loop(0, COLS)
        def _(blk):
            start = pl.multiple_of(blk * SLAB, SLAB)
            block = jnp.dot(hot[pl.ds(start, SLAB), :], rhs, preferred_element_type=F32)
            for u in range(n):
                xsend[blk, lo + u] = block[:, u * B:(u + 1) * B].astype(BF16)

        for dx, dc in ((1, 0), (3, 0), (1, 1), (3, 1), (2, 0), (2, 1), (0, 1)):
            to = ((x + dx) & 3) * 2 + ((core + dc) & 1)
            remote(
                xsend.at[to, pl.ds(lo, n)], xrecv.at[pl.ds(lo, n), col],
                cr_s, cr_r.at[chunk], at(row, to),
            ).start()

    def finish(chunk):
        lo, n = FROM[chunk], PARTS[chunk]
        part = pl.ds(lo, n)
        received(xrecv.at[part, pl.ds(0, COLS - 1)], cr_s, cr_r.at[chunk])
        for i in range(lo, lo + n):
            @pl.loop(0, 4)
            def _(q):
                lines = pl.ds(q * 32, 32)
                block = xsend[col, i, lines].astype(F32)
                for d in range(1, COLS):
                    block += xrecv[i, (col + d) & 7, lines].astype(F32)
                total[i, lines] = block

        for dy, dz in HOPS:
            to = ((y + dy) & 3) * 4 + ((z + dz) & 3)
            remote(
                total.at[part, pl.ds(pl.multiple_of(to * 8, 8), 8)],
                last.at[pl.ds(row * 8 + lo, n)],
                fin_s, fin_r, at(to, col),
            ).start()

        last[pl.ds(row * 8 + lo, n)] = total[part, pl.ds(pl.multiple_of(row * 8, 8), 8), :]

    for chunk in range(CHUNKS):
        received(recvbuf.at[pl.ds(FROM[chunk], PARTS[chunk]), pl.ds(0, ROWS - 1)], ex_s, ex_r.at[chunk])
        if chunk + 2 < CHUNKS:
            exchange(chunk + 2, 0, SLAB)
        scatter(chunk)
        if chunk > 0:
            finish(chunk - 1)
    finish(CHUNKS - 1)
    received(last.at[pl.ds(0, ROWS * 8 - 8)], fin_s, fin_r)
    for b in range(8):
        out_ref[b // 4, b % 4] = last[:, b, :]

    sent(panel.at[pl.ds(0, 240)], ag_s, ag_r.at[0])
    sent(own.at[pl.ds(0, 112)], x_s, x_r.at[0])
    sent(metas.at[pl.ds(0, ROWS - 1)], meta_s, meta_r)
    sent(sendbuf.at[pl.ds(0, 120)], ex_s, ex_r.at[0])
    sent(xsend.at[pl.ds(0, COLS - 1)], cr_s, cr_r.at[0])
    sent(last.at[pl.ds(0, ROWS * 8 - 8)], fin_s, fin_r)


def shards(a_blocks, p_tiles, owner, agg_local, a_cols):
    vmem = pl.BlockSpec(memory_space=pltpu.VMEM)
    dma = pltpu.SemaphoreType.DMA
    return pl.pallas_call(
        kernel,
        out_shape=jax.ShapeDtypeStruct((OWN, 4, B, B), F32),
        in_specs=[
            pl.BlockSpec(memory_space=pltpu.SMEM), vmem, vmem, vmem, vmem, pl.BlockSpec(memory_space=pl.ANY)
        ],
        out_specs=vmem,
        scratch_shapes=[
            pltpu.VMEM((SLAB, 1, B, B), BF16),
            pltpu.VMEM((ROWS * TPD, B, B), BF16),
            pltpu.VMEM((COLS * TPD, B, B), BF16),
            pltpu.VMEM((ROWS, 8, SLAB), jnp.int32),
            pltpu.VMEM((BLOCKS, ROWS * SLAB), BF16),
            pltpu.VMEM((GT * B, B), F32),
            pltpu.VMEM((B, SLAB, B), BF16),
            pltpu.VMEM((8, ROWS, SLAB, B), BF16),
            pltpu.VMEM((COLS, 8, SLAB, B), BF16),
            pltpu.VMEM((8, COLS, SLAB, B), BF16),
            pltpu.VMEM((8, SLAB, B), F32),
            pltpu.VMEM((ROWS * 8, 8, B), F32),
            dma, dma((9,)), dma, dma, dma, dma((25,)), dma, dma((8,)),
            dma, dma((CHUNKS,)), dma, dma((CHUNKS,)), dma, dma,
        ],
        compiler_params=pltpu.CompilerParams(
            collective_id=0, has_side_effects=True, vmem_limit_bytes=56 * 1024 * 1024
        ),
    )(
        a_cols.reshape(SLAB), owner.reshape(1, SLAB), agg_local.reshape(1, SLAB),
        a_cols.reshape(1, SLAB), p_tiles, a_blocks,
    )


def solution(mesh):
    in_specs = (
        P("row", "col", None, None),
        P(("row", "col"), None, None),
        P("row", None),
        P("row"),
        P("row", "col"),
    )
    out_specs = P("row", "col", None, None)
    return jax.shard_map(shards, mesh=mesh, in_specs=in_specs, out_specs=out_specs, check_vma=False)
```

```python
import functools

import jax
import jax.numpy as jnp
from jax import lax
from jax.experimental import pallas as pl
from jax.experimental.pallas import tpu as pltpu
from jax.sharding import PartitionSpec as P

MESH = pl.DeviceIdType.MESH
OWN = 2
B = 128
SIDE = 4
ROWS = 16
COLS = 8
TPD = 16
SLAB = 128
NAGG = 32
BLOCKS = NAGG * NAGG
GROUPS = 8
GT = SLAB // GROUPS
PARTS = (2, 2)
PARTS2 = (2, 2)
CHUNKS, CHUNKS2 = len(PARTS), len(PARTS2)
SPLIT = sum(PARTS)
REST = 8 - SPLIT
FROM = tuple(sum(PARTS[:n]) for n in range(CHUNKS))
FROM2 = tuple(sum(PARTS2[:n]) for n in range(CHUNKS2))
HOPS = (
    (1, 0), (3, 0), (0, 1), (0, 3), (1, 1), (3, 3), (1, 3), (3, 1),
    (2, 0), (0, 2), (2, 2), (1, 2), (2, 1), (3, 2), (2, 3),
)
ORDER = ("S0", "s0", "s1", "S1", "f0", "M0", "f1", "M1", "F0", "F1")
XHOPS = ((1, 0), (3, 0), (1, 1), (3, 1), (2, 0), (2, 1), (0, 1))
F32 = jnp.float32
BF16 = jnp.bfloat16


def iota(shape, dim):
    return lax.broadcasted_iota(jnp.int32, shape, dim)


def kernel(
    cols_ref, owner_ref, local_ref, tiles_ref, p_ref, a_hbm, out_ref,
    a_ref, panel, own, metas, slabs, hot, hot2, terms, sendbuf, recvbuf, xsend, xrecv, total,
    pieces, dense, part1, sum1, part2, sum2, last,
    a_sem, loc_sem, meta_s, meta_r, slab_s, slab_r, ag_s, ag_r, x_s, x_r, ex_s, ex_r, cr_s, cr_r, fin_s, fin_r,
    pc_s, pc_r, p1_s, p1_r, p2_s, p2_r, p3_s, p3_r,
):
    row = lax.axis_index("row")
    col = lax.axis_index("col")
    y, z = row >> 2, row & 3
    x, core = col >> 1, col & 1

    def at(r, c):
        return {"row": r, "col": c}

    def remote(src, dst, ss, rs, dev):
        return pltpu.make_async_remote_copy(
            src_ref=src, dst_ref=dst, send_sem=ss, recv_sem=rs, device_id=dev, device_id_type=MESH
        )

    def received(ref, ss, rs):
        remote(ref, ref, ss, rs, at(row, col)).wait_recv()

    def sent(ref, ss, rs):
        remote(ref, ref, ss, rs, at(row, col)).wait_send()

    right, left = ((x + 1) & 3) * 2 + core, ((x + 3) & 3) * 2 + core
    far = ((x + 2) & 3) * 2 + core
    sib = x * 2 + 1 - core

    barrier = pltpu.get_barrier_semaphore()
    near = [(((y + 1) & 3) * 4 + z, col), (((y + 3) & 3) * 4 + z, col), (y * 4 + ((z + 1) & 3), col),
            (y * 4 + ((z + 3) & 3), col), (row, right), (row, left), (row, sib)]
    for r, c in near:
        pl.semaphore_signal(barrier, inc=1, device_id=at(r, c), device_id_type=MESH)

    a_copy = pltpu.make_async_copy(a_hbm, a_ref, a_sem)
    a_copy.start()
    p_copy = pltpu.make_async_copy(p_ref, panel.at[pl.ds(row * TPD, TPD)], loc_sem.at[0])
    p_copy.start()
    mine = jnp.concatenate(
        [owner_ref[...] * OWN + local_ref[...], tiles_ref[...], jnp.zeros((6, SLAB), jnp.int32)], 0
    )
    metas[row] = mine
    slabs[col] = mine
    for w in range(TPD):
        own[col * TPD + w] = p_ref[w].T
    pl.semaphore_wait(barrier, len(near))

    class Half:
        sems = {}

        def __init__(self, h):
            self.h = h
            self.f, self.s = (y, z) if h == 0 else (z, y)

        def slot(self, df, ds):
            f, s = (self.f + df) & 3, (self.s + ds) & 3
            return f * SIDE + s if self.h == 0 else s * SIDE + f

        def sem(self, name):
            if name[:2] == "2f":
                return ag_r.at[0]
            return ag_r.at[Half.sems.setdefault((self.h, name), len(Half.sems) + 1)]

        def part(self, slot, lo, n):
            return panel.at[pl.ds(self.slot(*slot) * TPD + 8 * self.h + lo, n)]

        def send(self, name, slot, lo, n, to):
            src = p_ref.at[pl.ds(8 * self.h + lo, n)] if slot == (0, 0) else self.part(slot, lo, n)
            remote(src, self.part(slot, lo, n), ag_s, self.sem(name), at(self.slot(*to), col)).start()

        def recv(self, name, slot, lo, n):
            received(self.part(slot, lo, n), ag_s, self.sem(name))

    halves = [Half(0), Half(1)]
    for h in halves:
        h.send("1+", (0, 0), 0, 8, (1, 0))
        h.send("1-", (0, 0), 0, 8, (-1, 0))
    for h in halves:
        h.send("2+0", (0, 0), 0, 8, (0, 1))
        h.send("2-0", (0, 0), 0, 8, (0, -1))

    def own_send(k, c, lo, n, to):
        ref = own.at[pl.ds(c * TPD + lo, n)]
        remote(ref, ref, x_s, x_r.at[k], at(row, to)).start()

    def own_recv(k, c, lo, n):
        received(own.at[pl.ds(c * TPD + lo, n)], x_s, x_r.at[k])

    own_send(0, col, 0, TPD, right)
    own_send(1, col, 0, TPD, left)
    own_send(2, col, 0, TPD, sib)

    for h in halves:
        h.recv("1+", (-1, 0), 0, 8)
        h.send("1f+", (-1, 0), 0, 4, (1, 0))
        h.recv("1-", (1, 0), 0, 8)
        h.send("1f-", (1, 0), 4, 4, (-1, 0))
    for h in halves:
        for q in (-1, 1):
            h.send(f"2+{q}", (q, 0), 0, 8, (0, 1))
            h.send(f"2-{q}", (q, 0), 0, 8, (0, -1))

    def forward(q):
        for h in halves:
            h.recv(f"2+{q}", (q, -1), 0, 8)
            h.send("2f+", (q, -1), 0, 4, (0, 1))
            h.recv(f"2-{q}", (q, 1), 0, 8)
            h.send("2f-", (q, 1), 4, 4, (0, -1))

    forward(0)
    for h in halves:
        h.recv("1f+", (2, 0), 0, 4)
        h.recv("1f-", (2, 0), 4, 4)
        h.send("2+2", (2, 0), 0, 8, (0, 1))
        h.send("2-2", (2, 0), 0, 8, (0, -1))

    own_recv(0, left, 0, TPD)
    own_send(3, left, 0, 8, right)
    own_send(5, left, 0, TPD, sib)
    own_recv(1, right, 0, TPD)
    own_send(4, right, 8, 8, left)
    own_send(6, right, 0, TPD, sib)

    forward(-1)
    forward(1)
    own_recv(3, far, 0, 8)
    own_recv(4, far, 8, 8)
    own_send(7, far, 0, TPD, sib)
    forward(2)
    own_recv(2, sib, 0, TPD)
    for k, c in ((5, left), (6, right), (7, far)):
        own_recv(k, c + 1 - 2 * core, 0, TPD)
    p_copy.wait()
    a_copy.wait()
    received(panel.at[pl.ds(0, 64)], ag_s, ag_r.at[0])

    @pl.loop(1, ROWS)
    def _(d):
        remote(metas.at[row], metas.at[row], meta_s, meta_r, at((row + d) & 15, col)).start()

    for dx, dc in XHOPS:
        to = ((x + dx) & 3) * 2 + ((core + dc) & 1)
        remote(slabs.at[col], slabs.at[col], slab_s, slab_r, at(row, to)).start()

    def exchange(chunk, lo, n):
        part = pl.ds(FROM[chunk], PARTS[chunk])
        for dy, dz in HOPS:
            to = ((y + dy) & 3) * 4 + ((z + dz) & 3)
            remote(
                sendbuf.at[to, part, pl.ds(lo, n)], recvbuf.at[part, row, pl.ds(lo, n)],
                ex_s, ex_r.at[chunk], at(to, col),
            ).start()

    def exchange2(chunk, lo, n):
        for dx, dc in XHOPS:
            to = ((x + dx) & 3) * 2 + ((core + dc) & 1)
            remote(
                sendbuf.at[pl.ds(to * 2, 2), pl.ds(SPLIT + FROM2[chunk], PARTS2[chunk]), pl.ds(lo, n)],
                pieces.at[:, pl.ds(FROM2[chunk], PARTS2[chunk]), col, pl.ds(lo, n)],
                pc_s, pc_r.at[chunk], at(row, to),
            ).start()

    @pl.loop(0, GROUPS)
    def _(g):
        lo = pl.multiple_of(g * GT, GT)
        for u in range(GT):
            tile = cols_ref[lo + u]
            prod = jnp.dot(
                a_ref[lo + u, 0], panel[(tile >> 7) * TPD + (tile & 15)], preferred_element_type=F32
            ).astype(BF16)
            terms[u * B:(u + 1) * B, :] = jnp.dot(own[lo + u], prod, preferred_element_type=F32)

        @pl.loop(0, ROWS)
        def _(step):
            for u in range(8):
                sendbuf[step, u, pl.ds(lo, GT), :] = terms[
                    pl.ds(step * 8 + u, GT, stride=B), :
                ].astype(BF16)

        exchange2(0, lo, GT)
        exchange(0, lo, GT)

    for chunk in range(1, CHUNKS2):
        exchange2(chunk, 0, SLAB)
    for chunk in range(1, CHUNKS):
        exchange(chunk, 0, SLAB)
    own_copies = [
        pltpu.make_async_copy(sendbuf.at[row, i], recvbuf.at[i, row], loc_sem.at[1 + i])
        for i in range(SPLIT)
    ] + [
        pltpu.make_async_copy(
            sendbuf.at[col * 2 + h, SPLIT + i], pieces.at[h, i, col], loc_sem.at[1 + SPLIT + h * REST + i]
        )
        for h in range(2) for i in range(REST)
    ]
    for c in own_copies:
        c.start()

    received(metas.at[pl.ds(0, ROWS - 1)], meta_s, meta_r)
    received(slabs.at[pl.ds(0, COLS - 1)], slab_s, slab_r)
    aggs = jnp.concatenate([metas[r, 0:1, :] for r in range(ROWS)], 0).astype(F32).astype(BF16)

    def coarse_column(g):
        lane_hot = jnp.where(iota((SLAB, SLAB), 0) == (g & (SLAB - 1)), 1.0, 0.0).astype(BF16)
        picked = jnp.dot(aggs, lane_hot, preferred_element_type=F32)
        slab_hot = iota((ROWS, SLAB), 0) == (g >> 7)
        return jnp.sum(jnp.where(slab_hot, picked, 0.0), 0, keepdims=True).astype(jnp.int32)

    for c in range(COLS):
        big_j = coarse_column(slabs[c, 1:2, :])
        big_i = slabs[c, 0:1, :]
        dest = (big_i >> 1) * 64 + (big_j >> 2) * 8 + (big_i & 1) * 4 + (big_j & 3)
        for blk in range(COLS):
            hot2[blk * SLAB:(blk + 1) * SLAB, c * SLAB:(c + 1) * SLAB] = jnp.where(
                iota((SLAB, SLAB), 0) + blk * SLAB == dest, 1.0, 0.0
            ).astype(BF16)
    for r in range(ROWS):
        big_j = coarse_column(metas[r, 1:2, :])
        big_i = metas[r, 0:1, :]
        dest = (big_j >> 2) * SLAB + big_i * 4 + (big_j & 3)
        for blk in range(COLS):
            hot[blk * SLAB:(blk + 1) * SLAB, r * SLAB:(r + 1) * SLAB] = jnp.where(
                iota((SLAB, SLAB), 0) + blk * SLAB == dest, 1.0, 0.0
            ).astype(BF16)
    for c in own_copies:
        c.wait()

    def scatter(chunk):
        lo, n = FROM[chunk], PARTS[chunk]
        received(recvbuf.at[pl.ds(lo, n), pl.ds(0, ROWS - 1)], ex_s, ex_r.at[chunk])
        rhs = jnp.concatenate([recvbuf[lo + u].reshape(ROWS * SLAB, B) for u in range(n)], 1)

        @pl.loop(0, COLS)
        def _(blk):
            start = pl.multiple_of(blk * SLAB, SLAB)
            block = jnp.dot(hot[pl.ds(start, SLAB), :], rhs, preferred_element_type=F32)
            for u in range(n):
                xsend[blk, lo + u] = block[:, u * B:(u + 1) * B].astype(BF16)

        for dx, dc in XHOPS:
            to = ((x + dx) & 3) * 2 + ((core + dc) & 1)
            remote(
                xsend.at[to, pl.ds(lo, n)], xrecv.at[pl.ds(lo, n), col],
                cr_s, cr_r.at[chunk], at(row, to),
            ).start()

    def finish(chunk):
        lo, n = FROM[chunk], PARTS[chunk]
        part = pl.ds(lo, n)
        received(xrecv.at[part, pl.ds(0, COLS - 1)], cr_s, cr_r.at[chunk])
        for i in range(lo, lo + n):
            @pl.loop(0, 4)
            def _(q):
                lines = pl.ds(q * 32, 32)
                block = xsend[col, i, lines].astype(F32)
                for d in range(1, COLS):
                    block += xrecv[i, (col + d) & 7, lines].astype(F32)
                total[i, lines] = block

        for dy, dz in HOPS:
            to = ((y + dy) & 3) * 4 + ((z + dz) & 3)
            remote(
                total.at[part, pl.ds(pl.multiple_of(to * 8, 8), 8)], last.at[row, part],
                fin_s, fin_r, at(to, col),
            ).start()
        last[row, part] = total[part, pl.ds(pl.multiple_of(row * 8, 8), 8), :]

    def scatter2(chunk):
        lo, n = FROM2[chunk], PARTS2[chunk]
        part = pl.ds(lo, n)
        received(pieces.at[:, part, pl.ds(0, COLS - 1)], pc_s, pc_r.at[chunk])
        for h in range(2):
            rhs = jnp.concatenate([pieces[h, lo + u].reshape(COLS * SLAB, B) for u in range(n)], 1)

            @pl.loop(0, COLS)
            def _(blk):
                start = pl.multiple_of(blk * SLAB, SLAB)
                block = jnp.dot(hot2[pl.ds(start, SLAB), :], rhs, preferred_element_type=F32).astype(BF16)
                for u in range(n):
                    for v in range(2):
                        dense[h, lo + u, blk >> 1, (blk & 1) * 2 + v] = block[
                            v * 64:(v + 1) * 64, u * B:(u + 1) * B
                        ]

            for d in (1, 3, 2):
                if h == 0:
                    to = (y + d) & 3
                    src, here, dev = dense.at[0, part, to], y, to * 4 + z
                else:
                    to = (z + d) & 3
                    src, here, dev = dense.at[1, part, :, to], z, y * 4 + to
                remote(src, part1.at[h, part, here], p1_s, p1_r.at[chunk, h], at(dev, col)).start()

    def middle2(chunk):
        lo, n = FROM2[chunk], PARTS2[chunk]
        part = pl.ds(lo, n)
        for h in range(2):
            received(part1.at[h, part, pl.ds(0, 3)], p1_s, p1_r.at[chunk, h])
            here = y if h == 0 else z
            for i in range(lo, lo + n):
                for q in range(4):
                    block = (dense[0, i, y, q] if h == 0 else dense[1, i, q, z]).astype(F32)
                    for d in (1, 2, 3):
                        block += part1[h, i, (here + d) & 3, q].astype(F32)
                    sum1[h, i, q] = block
            for d in (1, 3, 2):
                if h == 0:
                    to = (z + d) & 3
                    here2, dev = z, y * 4 + to
                else:
                    to = (y + d) & 3
                    here2, dev = y, to * 4 + z
                remote(
                    sum1.at[h, part, to], part2.at[h, part, here2], p2_s, p2_r.at[chunk, h], at(dev, col)
                ).start()

    def finish2(chunk):
        lo, n = FROM2[chunk], PARTS2[chunk]
        part = pl.ds(lo, n)
        for h in range(2):
            received(part2.at[h, part, pl.ds(0, 3)], p2_s, p2_r.at[chunk, h])
            here = z if h == 0 else y
            for i in range(lo, lo + n):
                block = sum1[h, i, here]
                for d in (1, 2, 3):
                    block += part2[h, i, (here + d) & 3]
                sum2[h, i] = block.reshape(COLS, 8, B)
        for dx, dc in XHOPS:
            to = ((x + dx) & 3) * 2 + ((core + dc) & 1)
            remote(
                sum2.at[:, part, to], last.at[pl.ds(col * 2, 2), pl.ds(SPLIT + lo, n)],
                p3_s, p3_r, at(row, to),
            ).start()
        for h in range(2):
            for i in range(lo, lo + n):
                last[col * 2 + h, SPLIT + i] = sum2[h, i, col]

    for step in ORDER:
        {"s": scatter, "f": finish, "S": scatter2, "M": middle2, "F": finish2}[step[0]](int(step[1]))
    received(last.at[pl.ds(0, ROWS - 1), pl.ds(0, SPLIT)], fin_s, fin_r)
    received(last.at[pl.ds(0, ROWS - 2), pl.ds(SPLIT, REST)], p3_s, p3_r)
    for b in range(8):
        out_ref[b // 4, b % 4] = last[:, :, b, :].reshape(B, B)

    sent(panel.at[pl.ds(0, 240)], ag_s, ag_r.at[0])
    sent(own.at[pl.ds(0, 112)], x_s, x_r.at[0])
    sent(metas.at[pl.ds(0, ROWS - 1)], meta_s, meta_r)
    sent(slabs.at[pl.ds(0, COLS - 1)], slab_s, slab_r)
    sent(sendbuf.at[pl.ds(0, ROWS - 1), pl.ds(0, SPLIT)], ex_s, ex_r.at[0])
    sent(sendbuf.at[pl.ds(0, ROWS - 2), pl.ds(SPLIT, REST)], pc_s, pc_r.at[0])
    sent(xsend.at[pl.ds(0, COLS - 1)], cr_s, cr_r.at[0])
    sent(last.at[pl.ds(0, ROWS - 1), pl.ds(0, SPLIT)], fin_s, fin_r)
    sent(dense.at[:, :, pl.ds(0, 3)], p1_s, p1_r.at[0, 0])
    sent(sum1.at[:, :, pl.ds(0, 3)], p2_s, p2_r.at[0, 0])
    sent(sum2.at[:, :, pl.ds(0, COLS - 1)], p3_s, p3_r)


def shards(a_blocks, p_tiles, owner, agg_local, a_cols):
    vmem = pl.BlockSpec(memory_space=pltpu.VMEM)
    dma = pltpu.SemaphoreType.DMA
    return pl.pallas_call(
        kernel,
        out_shape=jax.ShapeDtypeStruct((OWN, 4, B, B), F32),
        in_specs=[
            pl.BlockSpec(memory_space=pltpu.SMEM), vmem, vmem, vmem, vmem, pl.BlockSpec(memory_space=pl.ANY)
        ],
        out_specs=vmem,
        scratch_shapes=[
            pltpu.VMEM((SLAB, 1, B, B), BF16),
            pltpu.VMEM((ROWS * TPD, B, B), BF16),
            pltpu.VMEM((COLS * TPD, B, B), BF16),
            pltpu.VMEM((ROWS, 8, SLAB), jnp.int32),
            pltpu.VMEM((COLS, 8, SLAB), jnp.int32),
            pltpu.VMEM((BLOCKS, ROWS * SLAB), BF16),
            pltpu.VMEM((BLOCKS, COLS * SLAB), BF16),
            pltpu.VMEM((GT * B, B), F32),
            pltpu.VMEM((ROWS, 8, SLAB, B), BF16),
            pltpu.VMEM((SPLIT, ROWS, SLAB, B), BF16),
            pltpu.VMEM((COLS, SPLIT, SLAB, B), BF16),
            pltpu.VMEM((SPLIT, COLS, SLAB, B), BF16),
            pltpu.VMEM((SPLIT, SLAB, B), F32),
            pltpu.VMEM((2, REST, COLS, SLAB, B), BF16),
            pltpu.VMEM((2, REST, 4, 4, 64, B), BF16),
            pltpu.VMEM((2, REST, 4, 4, 64, B), BF16),
            pltpu.VMEM((2, REST, 4, 64, B), F32),
            pltpu.VMEM((2, REST, 4, 64, B), F32),
            pltpu.VMEM((2, REST, COLS, 8, B), F32),
            pltpu.VMEM((ROWS, 8, 8, B), F32),
            dma, dma((1 + SPLIT + 2 * REST,)), dma, dma, dma, dma, dma, dma((25,)), dma, dma((8,)),
            dma, dma((CHUNKS,)), dma, dma((CHUNKS,)), dma, dma,
            dma, dma((CHUNKS2,)), dma, dma((CHUNKS2, 2)), dma, dma((CHUNKS2, 2)), dma, dma,
        ],
        compiler_params=pltpu.CompilerParams(
            collective_id=0, has_side_effects=True, vmem_limit_bytes=56 * 1024 * 1024
        ),
    )(
        a_cols.reshape(SLAB), owner.reshape(1, SLAB), agg_local.reshape(1, SLAB),
        a_cols.reshape(1, SLAB), p_tiles, a_blocks,
    )


def solution(mesh):
    in_specs = (
        P("row", "col", None, None),
        P(("row", "col"), None, None),
        P("row", None),
        P("row"),
        P("row", "col"),
    )
    out_specs = P("row", "col", None, None)
    return jax.shard_map(shards, mesh=mesh, in_specs=in_specs, out_specs=out_specs, check_vma=False)
```

```python
import functools

import jax
import jax.numpy as jnp
from jax import lax
from jax.experimental import pallas as pl
from jax.experimental.pallas import tpu as pltpu
from jax.sharding import PartitionSpec as P

MESH = pl.DeviceIdType.MESH
OWN = 2
B = 128
SIDE = 4
ROWS = 16
COLS = 8
TPD = 16
SLAB = 128
NAGG = 32
BLOCKS = NAGG * NAGG
GROUPS = 8
GT = SLAB // GROUPS
PARTS = (2, 2)
PARTS2 = (2, 2)
CHUNKS, CHUNKS2 = len(PARTS), len(PARTS2)
SPLIT = sum(PARTS)
REST = 8 - SPLIT
FROM = tuple(sum(PARTS[:n]) for n in range(CHUNKS))
FROM2 = tuple(sum(PARTS2[:n]) for n in range(CHUNKS2))
HOPS = (
    (1, 0), (3, 0), (0, 1), (0, 3), (1, 1), (3, 3), (1, 3), (3, 1),
    (2, 0), (0, 2), (2, 2), (1, 2), (2, 1), (3, 2), (2, 3),
)
ORDER = ('s0', 'S0', 'S1', 'M0', 'f0', 's1', 'M1', 'F0', 'f1', 'F1')
XHOPS = ((1, 0), (3, 0), (1, 1), (3, 1), (2, 0), (2, 1), (0, 1))
F32 = jnp.float32
BF16 = jnp.bfloat16


def iota(shape, dim):
    return lax.broadcasted_iota(jnp.int32, shape, dim)


def kernel(
    cols_ref, owner_ref, local_ref, tiles_ref, p_ref, a_hbm, out_ref,
    a_ref, panel, own, metas, slabs, hot, hot2, terms, sendbuf, recvbuf, xsend, xrecv, total,
    pieces, dense, part1, sum1, part2, sum2, last,
    a_sem, loc_sem, meta_s, meta_r, slab_s, slab_r, ag_s, ag_r, x_s, x_r, ex_s, ex_r, cr_s, cr_r, fin_s, fin_r,
    pc_s, pc_r, p1_s, p1_r, p2_s, p2_r, p3_s, p3_r,
):
    row = lax.axis_index("row")
    col = lax.axis_index("col")
    y, z = row >> 2, row & 3
    x, core = col >> 1, col & 1

    def at(r, c):
        return {"row": r, "col": c}

    def remote(src, dst, ss, rs, dev):
        return pltpu.make_async_remote_copy(
            src_ref=src, dst_ref=dst, send_sem=ss, recv_sem=rs, device_id=dev, device_id_type=MESH
        )

    def received(ref, ss, rs):
        remote(ref, ref, ss, rs, at(row, col)).wait_recv()

    def sent(ref, ss, rs):
        remote(ref, ref, ss, rs, at(row, col)).wait_send()

    right, left = ((x + 1) & 3) * 2 + core, ((x + 3) & 3) * 2 + core
    far = ((x + 2) & 3) * 2 + core
    sib = x * 2 + 1 - core

    barrier = pltpu.get_barrier_semaphore()
    near = [(((y + 1) & 3) * 4 + z, col), (((y + 3) & 3) * 4 + z, col), (y * 4 + ((z + 1) & 3), col),
            (y * 4 + ((z + 3) & 3), col), (row, right), (row, left), (row, sib)]
    for r, c in near:
        pl.semaphore_signal(barrier, inc=1, device_id=at(r, c), device_id_type=MESH)

    a_copy = pltpu.make_async_copy(a_hbm, a_ref, a_sem)
    a_copy.start()
    p_copy = pltpu.make_async_copy(p_ref, panel.at[pl.ds(row * TPD, TPD)], loc_sem.at[0])
    p_copy.start()
    mine = jnp.concatenate(
        [owner_ref[...] * OWN + local_ref[...], tiles_ref[...], jnp.zeros((6, SLAB), jnp.int32)], 0
    )
    metas[row] = mine
    slabs[col] = mine
    pl.semaphore_wait(barrier, len(near))

    class Half:
        sems = {}

        def __init__(self, h):
            self.h = h
            self.f, self.s = (y, z) if h == 0 else (z, y)

        def slot(self, df, ds):
            f, s = (self.f + df) & 3, (self.s + ds) & 3
            return f * SIDE + s if self.h == 0 else s * SIDE + f

        def sem(self, name):
            if name[:2] == "2f":
                return ag_r.at[0]
            return ag_r.at[Half.sems.setdefault((self.h, name), len(Half.sems) + 1)]

        def part(self, slot, lo, n):
            return panel.at[pl.ds(self.slot(*slot) * TPD + 8 * self.h + lo, n)]

        def send(self, name, slot, lo, n, to):
            src = p_ref.at[pl.ds(8 * self.h + lo, n)] if slot == (0, 0) else self.part(slot, lo, n)
            remote(src, self.part(slot, lo, n), ag_s, self.sem(name), at(self.slot(*to), col)).start()

        def recv(self, name, slot, lo, n):
            received(self.part(slot, lo, n), ag_s, self.sem(name))

    halves = [Half(0), Half(1)]
    for h in halves:
        h.send("1+", (0, 0), 0, 8, (1, 0))
        h.send("1-", (0, 0), 0, 8, (-1, 0))
    for h in halves:
        h.send("2+0", (0, 0), 0, 8, (0, 1))
        h.send("2-0", (0, 0), 0, 8, (0, -1))

    p_copy.wait()
    for w in range(TPD):
        own[col * TPD + w] = panel[row * TPD + w].T
    def own_send(k, c, lo, n, to):
        ref = own.at[pl.ds(c * TPD + lo, n)]
        remote(ref, ref, x_s, x_r.at[k], at(row, to)).start()

    def own_recv(k, c, lo, n):
        received(own.at[pl.ds(c * TPD + lo, n)], x_s, x_r.at[k])

    own_send(0, col, 0, TPD, right)
    own_send(1, col, 0, TPD, left)
    own_send(2, col, 0, TPD, sib)

    for h in halves:
        h.recv("1+", (-1, 0), 0, 8)
        h.send("1f+", (-1, 0), 0, 4, (1, 0))
        h.recv("1-", (1, 0), 0, 8)
        h.send("1f-", (1, 0), 4, 4, (-1, 0))
    for h in halves:
        for q in (-1, 1):
            h.send(f"2+{q}", (q, 0), 0, 8, (0, 1))
            h.send(f"2-{q}", (q, 0), 0, 8, (0, -1))

    def forward(q):
        for h in halves:
            h.recv(f"2+{q}", (q, -1), 0, 8)
            h.send("2f+", (q, -1), 0, 4, (0, 1))
            h.recv(f"2-{q}", (q, 1), 0, 8)
            h.send("2f-", (q, 1), 4, 4, (0, -1))

    forward(0)
    for h in halves:
        h.recv("1f+", (2, 0), 0, 4)
        h.recv("1f-", (2, 0), 4, 4)
        h.send("2+2", (2, 0), 0, 8, (0, 1))
        h.send("2-2", (2, 0), 0, 8, (0, -1))

    own_recv(0, left, 0, TPD)
    own_send(3, left, 0, 8, right)
    own_send(5, left, 0, TPD, sib)
    own_recv(1, right, 0, TPD)
    own_send(4, right, 8, 8, left)
    own_send(6, right, 0, TPD, sib)

    forward(-1)
    forward(1)
    own_recv(3, far, 0, 8)
    own_recv(4, far, 8, 8)
    own_send(7, far, 0, TPD, sib)
    forward(2)
    own_recv(2, sib, 0, TPD)
    for k, c in ((5, left), (6, right), (7, far)):
        own_recv(k, c + 1 - 2 * core, 0, TPD)
    a_copy.wait()
    received(panel.at[pl.ds(0, 64)], ag_s, ag_r.at[0])

    @pl.loop(1, ROWS)
    def _(d):
        remote(metas.at[row], metas.at[row], meta_s, meta_r, at((row + d) & 15, col)).start()

    for dx, dc in XHOPS:
        to = ((x + dx) & 3) * 2 + ((core + dc) & 1)
        remote(slabs.at[col], slabs.at[col], slab_s, slab_r, at(row, to)).start()

    def exchange(chunk, lo, n):
        part = pl.ds(FROM[chunk], PARTS[chunk])
        for dy, dz in HOPS:
            to = ((y + dy) & 3) * 4 + ((z + dz) & 3)
            remote(
                sendbuf.at[to, part, pl.ds(lo, n)], recvbuf.at[part, row, pl.ds(lo, n)],
                ex_s, ex_r.at[chunk], at(to, col),
            ).start()

    def exchange2(chunk, lo, n):
        for dx, dc in XHOPS:
            to = ((x + dx) & 3) * 2 + ((core + dc) & 1)
            remote(
                sendbuf.at[pl.ds(to * 2, 2), pl.ds(SPLIT + FROM2[chunk], PARTS2[chunk]), pl.ds(lo, n)],
                pieces.at[:, pl.ds(FROM2[chunk], PARTS2[chunk]), col, pl.ds(lo, n)],
                pc_s, pc_r.at[chunk], at(row, to),
            ).start()

    @pl.loop(0, GROUPS)
    def _(g):
        lo = pl.multiple_of(g * GT, GT)
        for u in range(GT):
            tile = cols_ref[lo + u]
            prod = jnp.dot(
                a_ref[lo + u, 0], panel[(tile >> 7) * TPD + (tile & 15)], preferred_element_type=F32
            ).astype(BF16)
            terms[u * B:(u + 1) * B, :] = jnp.dot(own[lo + u], prod, preferred_element_type=F32)

        @pl.loop(0, ROWS)
        def _(step):
            for u in range(8):
                sendbuf[step, u, pl.ds(lo, GT), :] = terms[
                    pl.ds(step * 8 + u, GT, stride=B), :
                ].astype(BF16)

        exchange2(0, lo, GT)
        exchange(0, lo, GT)

    for chunk in range(1, CHUNKS2):
        exchange2(chunk, 0, SLAB)
    for chunk in range(1, CHUNKS):
        exchange(chunk, 0, SLAB)
    own_copies = [
        pltpu.make_async_copy(sendbuf.at[row, i], recvbuf.at[i, row], loc_sem.at[1 + i])
        for i in range(SPLIT)
    ] + [
        pltpu.make_async_copy(
            sendbuf.at[col * 2 + h, SPLIT + i], pieces.at[h, i, col], loc_sem.at[1 + SPLIT + h * REST + i]
        )
        for h in range(2) for i in range(REST)
    ]
    for c in own_copies:
        c.start()

    received(metas.at[pl.ds(0, ROWS - 1)], meta_s, meta_r)
    received(slabs.at[pl.ds(0, COLS - 1)], slab_s, slab_r)
    aggs = jnp.concatenate([metas[r, 0:1, :] for r in range(ROWS)], 0).astype(F32).astype(BF16)

    def coarse_column(g):
        lane_hot = jnp.where(iota((SLAB, SLAB), 0) == (g & (SLAB - 1)), 1.0, 0.0).astype(BF16)
        picked = jnp.dot(aggs, lane_hot, preferred_element_type=F32)
        slab_hot = iota((ROWS, SLAB), 0) == (g >> 7)
        return jnp.sum(jnp.where(slab_hot, picked, 0.0), 0, keepdims=True).astype(jnp.int32)

    for c in range(COLS):
        big_j = coarse_column(slabs[c, 1:2, :])
        big_i = slabs[c, 0:1, :]
        dest = (big_i >> 1) * 64 + (big_j >> 2) * 8 + (big_i & 1) * 4 + (big_j & 3)
        for blk in range(COLS):
            hot2[blk * SLAB:(blk + 1) * SLAB, c * SLAB:(c + 1) * SLAB] = jnp.where(
                iota((SLAB, SLAB), 0) + blk * SLAB == dest, 1.0, 0.0
            ).astype(BF16)
    for r in range(ROWS):
        big_j = coarse_column(metas[r, 1:2, :])
        big_i = metas[r, 0:1, :]
        dest = (big_j >> 2) * SLAB + big_i * 4 + (big_j & 3)
        for blk in range(COLS):
            hot[blk * SLAB:(blk + 1) * SLAB, r * SLAB:(r + 1) * SLAB] = jnp.where(
                iota((SLAB, SLAB), 0) + blk * SLAB == dest, 1.0, 0.0
            ).astype(BF16)
    for c in own_copies:
        c.wait()

    def scatter(chunk):
        lo, n = FROM[chunk], PARTS[chunk]
        received(recvbuf.at[pl.ds(lo, n), pl.ds(0, ROWS - 1)], ex_s, ex_r.at[chunk])
        rhs = jnp.concatenate([recvbuf[lo + u].reshape(ROWS * SLAB, B) for u in range(n)], 1)

        @pl.loop(0, COLS)
        def _(blk):
            start = pl.multiple_of(blk * SLAB, SLAB)
            block = jnp.dot(hot[pl.ds(start, SLAB), :], rhs, preferred_element_type=F32)
            for u in range(n):
                xsend[blk, lo + u] = block[:, u * B:(u + 1) * B].astype(BF16)

        for dx, dc in XHOPS:
            to = ((x + dx) & 3) * 2 + ((core + dc) & 1)
            remote(
                xsend.at[to, pl.ds(lo, n)], xrecv.at[pl.ds(lo, n), col],
                cr_s, cr_r.at[chunk], at(row, to),
            ).start()

    def finish(chunk):
        lo, n = FROM[chunk], PARTS[chunk]
        part = pl.ds(lo, n)
        received(xrecv.at[part, pl.ds(0, COLS - 1)], cr_s, cr_r.at[chunk])
        for i in range(lo, lo + n):
            @pl.loop(0, 4)
            def _(q):
                lines = pl.ds(q * 32, 32)
                block = xsend[col, i, lines].astype(F32)
                for d in range(1, COLS):
                    block += xrecv[i, (col + d) & 7, lines].astype(F32)
                total[i, lines] = block

        for dy, dz in HOPS:
            to = ((y + dy) & 3) * 4 + ((z + dz) & 3)
            remote(
                total.at[part, pl.ds(pl.multiple_of(to * 8, 8), 8)], last.at[row, part],
                fin_s, fin_r, at(to, col),
            ).start()
        last[row, part] = total[part, pl.ds(pl.multiple_of(row * 8, 8), 8), :]

    def scatter2(chunk):
        lo, n = FROM2[chunk], PARTS2[chunk]
        part = pl.ds(lo, n)
        received(pieces.at[:, part, pl.ds(0, COLS - 1)], pc_s, pc_r.at[chunk])
        for h in range(2):
            rhs = jnp.concatenate([pieces[h, lo + u].reshape(COLS * SLAB, B) for u in range(n)], 1)

            @pl.loop(0, COLS)
            def _(blk):
                start = pl.multiple_of(blk * SLAB, SLAB)
                block = jnp.dot(hot2[pl.ds(start, SLAB), :], rhs, preferred_element_type=F32).astype(BF16)
                for u in range(n):
                    for v in range(2):
                        dense[h, lo + u, blk >> 1, (blk & 1) * 2 + v] = block[
                            v * 64:(v + 1) * 64, u * B:(u + 1) * B
                        ]

            for d in (1, 3, 2):
                if h == 0:
                    to = (y + d) & 3
                    src, here, dev = dense.at[0, part, to], y, to * 4 + z
                else:
                    to = (z + d) & 3
                    src, here, dev = dense.at[1, part, :, to], z, y * 4 + to
                remote(src, part1.at[h, part, here], p1_s, p1_r.at[chunk, h], at(dev, col)).start()

    def middle2(chunk):
        lo, n = FROM2[chunk], PARTS2[chunk]
        part = pl.ds(lo, n)
        for h in range(2):
            received(part1.at[h, part, pl.ds(0, 3)], p1_s, p1_r.at[chunk, h])
            here = y if h == 0 else z
            for i in range(lo, lo + n):
                for q in range(4):
                    block = (dense[0, i, y, q] if h == 0 else dense[1, i, q, z]).astype(F32)
                    for d in (1, 2, 3):
                        block += part1[h, i, (here + d) & 3, q].astype(F32)
                    sum1[h, i, q] = block
            for d in (1, 3, 2):
                if h == 0:
                    to = (z + d) & 3
                    here2, dev = z, y * 4 + to
                else:
                    to = (y + d) & 3
                    here2, dev = y, to * 4 + z
                remote(
                    sum1.at[h, part, to], part2.at[h, part, here2], p2_s, p2_r.at[chunk, h], at(dev, col)
                ).start()

    def finish2(chunk):
        lo, n = FROM2[chunk], PARTS2[chunk]
        part = pl.ds(lo, n)
        for h in range(2):
            received(part2.at[h, part, pl.ds(0, 3)], p2_s, p2_r.at[chunk, h])
            here = z if h == 0 else y
            for i in range(lo, lo + n):
                block = sum1[h, i, here]
                for d in (1, 2, 3):
                    block += part2[h, i, (here + d) & 3]
                sum2[h, i] = block.reshape(COLS, 8, B)
        for dx, dc in XHOPS:
            to = ((x + dx) & 3) * 2 + ((core + dc) & 1)
            remote(
                sum2.at[:, part, to], last.at[pl.ds(col * 2, 2), pl.ds(SPLIT + lo, n)],
                p3_s, p3_r, at(row, to),
            ).start()
        for h in range(2):
            for i in range(lo, lo + n):
                last[col * 2 + h, SPLIT + i] = sum2[h, i, col]

    for step in ORDER:
        {"s": scatter, "f": finish, "S": scatter2, "M": middle2, "F": finish2}[step[0]](int(step[1]))
    received(last.at[pl.ds(0, ROWS - 1), pl.ds(0, SPLIT)], fin_s, fin_r)
    received(last.at[pl.ds(0, ROWS - 2), pl.ds(SPLIT, REST)], p3_s, p3_r)
    out_ref[...] = last[...]

    sent(panel.at[pl.ds(0, 240)], ag_s, ag_r.at[0])
    sent(own.at[pl.ds(0, 112)], x_s, x_r.at[0])
    sent(metas.at[pl.ds(0, ROWS - 1)], meta_s, meta_r)
    sent(slabs.at[pl.ds(0, COLS - 1)], slab_s, slab_r)
    sent(sendbuf.at[pl.ds(0, ROWS - 1), pl.ds(0, SPLIT)], ex_s, ex_r.at[0])
    sent(sendbuf.at[pl.ds(0, ROWS - 2), pl.ds(SPLIT, REST)], pc_s, pc_r.at[0])
    sent(xsend.at[pl.ds(0, COLS - 1)], cr_s, cr_r.at[0])
    sent(last.at[pl.ds(0, ROWS - 1), pl.ds(0, SPLIT)], fin_s, fin_r)
    sent(dense.at[:, :, pl.ds(0, 3)], p1_s, p1_r.at[0, 0])
    sent(sum1.at[:, :, pl.ds(0, 3)], p2_s, p2_r.at[0, 0])
    sent(sum2.at[:, :, pl.ds(0, COLS - 1)], p3_s, p3_r)


def shards(a_blocks, p_tiles, owner, agg_local, a_cols):
    vmem = pl.BlockSpec(memory_space=pltpu.VMEM)
    dma = pltpu.SemaphoreType.DMA
    rows = pl.pallas_call(
        kernel,
        out_shape=jax.ShapeDtypeStruct((ROWS, 8, 8, B), F32),
        in_specs=[
            pl.BlockSpec(memory_space=pltpu.SMEM), vmem, vmem, vmem, pl.BlockSpec(memory_space=pl.ANY), pl.BlockSpec(memory_space=pl.ANY)
        ],
        out_specs=vmem,
        scratch_shapes=[
            pltpu.VMEM((SLAB, 1, B, B), BF16),
            pltpu.VMEM((ROWS * TPD, B, B), BF16),
            pltpu.VMEM((COLS * TPD, B, B), BF16),
            pltpu.VMEM((ROWS, 8, SLAB), jnp.int32),
            pltpu.VMEM((COLS, 8, SLAB), jnp.int32),
            pltpu.VMEM((BLOCKS, ROWS * SLAB), BF16),
            pltpu.VMEM((BLOCKS, COLS * SLAB), BF16),
            pltpu.VMEM((GT * B, B), F32),
            pltpu.VMEM((ROWS, 8, SLAB, B), BF16),
            pltpu.VMEM((SPLIT, ROWS, SLAB, B), BF16),
            pltpu.VMEM((COLS, SPLIT, SLAB, B), BF16),
            pltpu.VMEM((SPLIT, COLS, SLAB, B), BF16),
            pltpu.VMEM((SPLIT, SLAB, B), F32),
            pltpu.VMEM((2, REST, COLS, SLAB, B), BF16),
            pltpu.VMEM((2, REST, 4, 4, 64, B), BF16),
            pltpu.VMEM((2, REST, 4, 4, 64, B), BF16),
            pltpu.VMEM((2, REST, 4, 64, B), F32),
            pltpu.VMEM((2, REST, 4, 64, B), F32),
            pltpu.VMEM((2, REST, COLS, 8, B), F32),
            pltpu.VMEM((ROWS, 8, 8, B), F32),
            dma, dma((1 + SPLIT + 2 * REST,)), dma, dma, dma, dma, dma, dma((25,)), dma, dma((8,)),
            dma, dma((CHUNKS,)), dma, dma((CHUNKS,)), dma, dma,
            dma, dma((CHUNKS2,)), dma, dma((CHUNKS2, 2)), dma, dma((CHUNKS2, 2)), dma, dma,
        ],
        compiler_params=pltpu.CompilerParams(
            collective_id=0, has_side_effects=True, vmem_limit_bytes=56 * 1024 * 1024
        ),
    )(
        a_cols.reshape(SLAB), owner.reshape(1, SLAB), agg_local.reshape(1, SLAB),
        a_cols.reshape(1, SLAB), p_tiles, a_blocks,
    )
    return rows.reshape(B, OWN, 4, B).transpose(1, 2, 0, 3)


def solution(mesh):
    in_specs = (
        P("row", "col", None, None),
        P(("row", "col"), None, None),
        P("row", None),
        P("row"),
        P("row", "col"),
    )
    out_specs = P("row", "col", None, None)
    return jax.shard_map(shards, mesh=mesh, in_specs=in_specs, out_specs=out_specs, check_vma=False)
```

```python
import functools

import jax
import jax.numpy as jnp
from jax import lax
from jax.experimental import pallas as pl
from jax.experimental.pallas import tpu as pltpu
from jax.sharding import PartitionSpec as P

MESH = pl.DeviceIdType.MESH
OWN = 2
B = 128
SIDE = 4
ROWS = 16
COLS = 8
TPD = 16
SLAB = 128
NAGG = 32
BLOCKS = NAGG * NAGG
GROUPS = 8
GT = SLAB // GROUPS
PARTS = (2, 2)
PARTS2 = (2, 2)
CHUNKS, CHUNKS2 = len(PARTS), len(PARTS2)
SPLIT = sum(PARTS)
REST = 8 - SPLIT
FROM = tuple(sum(PARTS[:n]) for n in range(CHUNKS))
FROM2 = tuple(sum(PARTS2[:n]) for n in range(CHUNKS2))
HOPS = (
    (1, 0), (3, 0), (0, 1), (0, 3), (1, 1), (3, 3), (1, 3), (3, 1),
    (2, 0), (0, 2), (2, 2), (1, 2), (2, 1), (3, 2), (2, 3),
)
ORDER = ('S0', 's0', 'S1', 's1', 'M0', 'M1', 'f0', 'F0', 'f1', 'F1')
XHOPS = ((1, 0), (3, 0), (1, 1), (3, 1), (2, 0), (2, 1), (0, 1))
F32 = jnp.float32
BF16 = jnp.bfloat16


def iota(shape, dim):
    return lax.broadcasted_iota(jnp.int32, shape, dim)


def kernel(
    cols_ref, owner_ref, local_ref, tiles_ref, p_ref, a_hbm, out_ref,
    a_ref, panel, own, metas, slabs, hot, hot2, terms, sendbuf, recvbuf, xsend, xrecv, total,
    pieces, dense, wide, part1, sum1, lean, part2, sum2,
    a_sem, loc_sem, meta_s, meta_r, slab_s, slab_r, ag_s, ag_r, x_s, x_r, ex_s, ex_r, cr_s, cr_r, fin_s, fin_r,
    pc_s, pc_r, p1_s, p1_r, p2_s, p2_r, p3_s, p3_r,
):
    last = out_ref
    row = lax.axis_index("row")
    col = lax.axis_index("col")
    y, z = row >> 2, row & 3
    x, core = col >> 1, col & 1

    def at(r, c):
        return {"row": r, "col": c}

    def remote(src, dst, ss, rs, dev):
        return pltpu.make_async_remote_copy(
            src_ref=src, dst_ref=dst, send_sem=ss, recv_sem=rs, device_id=dev, device_id_type=MESH
        )

    def received(ref, ss, rs):
        remote(ref, ref, ss, rs, at(row, col)).wait_recv()

    def sent(ref, ss, rs):
        remote(ref, ref, ss, rs, at(row, col)).wait_send()

    right, left = ((x + 1) & 3) * 2 + core, ((x + 3) & 3) * 2 + core
    far = ((x + 2) & 3) * 2 + core
    sib = x * 2 + 1 - core

    barrier = pltpu.get_barrier_semaphore()
    near = [(((y + 1) & 3) * 4 + z, col), (((y + 3) & 3) * 4 + z, col), (y * 4 + ((z + 1) & 3), col),
            (y * 4 + ((z + 3) & 3), col), (row, right), (row, left), (row, sib)]
    for r, c in near:
        pl.semaphore_signal(barrier, inc=1, device_id=at(r, c), device_id_type=MESH)

    a_copy = pltpu.make_async_copy(a_hbm, a_ref, a_sem)
    a_copy.start()
    p_copy = pltpu.make_async_copy(p_ref, panel.at[pl.ds(row * TPD, TPD)], loc_sem.at[0])
    p_copy.start()
    mine = jnp.concatenate(
        [owner_ref[...] * OWN + local_ref[...], tiles_ref[...], jnp.zeros((6, SLAB), jnp.int32)], 0
    )
    metas[row] = mine
    slabs[col] = mine
    pl.semaphore_wait(barrier, len(near))

    class Half:
        sems = {}

        def __init__(self, h):
            self.h = h
            self.f, self.s = (y, z) if h == 0 else (z, y)

        def slot(self, df, ds):
            f, s = (self.f + df) & 3, (self.s + ds) & 3
            return f * SIDE + s if self.h == 0 else s * SIDE + f

        def sem(self, name):
            if name[:2] == "2f":
                return ag_r.at[0]
            return ag_r.at[Half.sems.setdefault((self.h, name), len(Half.sems) + 1)]

        def part(self, slot, lo, n):
            return panel.at[pl.ds(self.slot(*slot) * TPD + 8 * self.h + lo, n)]

        def send(self, name, slot, lo, n, to):
            src = p_ref.at[pl.ds(8 * self.h + lo, n)] if slot == (0, 0) else self.part(slot, lo, n)
            remote(src, self.part(slot, lo, n), ag_s, self.sem(name), at(self.slot(*to), col)).start()

        def recv(self, name, slot, lo, n):
            received(self.part(slot, lo, n), ag_s, self.sem(name))

    halves = [Half(0), Half(1)]
    for h in halves:
        h.send("1+", (0, 0), 0, 8, (1, 0))
        h.send("1-", (0, 0), 0, 8, (-1, 0))
    for h in halves:
        h.send("2+0", (0, 0), 0, 8, (0, 1))
        h.send("2-0", (0, 0), 0, 8, (0, -1))

    p_copy.wait()
    for w in range(TPD):
        own[col * TPD + w] = panel[row * TPD + w].T
    def own_send(k, c, lo, n, to):
        ref = own.at[pl.ds(c * TPD + lo, n)]
        remote(ref, ref, x_s, x_r.at[k], at(row, to)).start()

    def own_recv(k, c, lo, n):
        received(own.at[pl.ds(c * TPD + lo, n)], x_s, x_r.at[k])

    own_send(0, col, 0, TPD, right)
    own_send(1, col, 0, TPD, left)
    own_send(2, col, 0, TPD, sib)

    for h in halves:
        h.recv("1+", (-1, 0), 0, 8)
        h.send("1f+", (-1, 0), 0, 4, (1, 0))
        h.recv("1-", (1, 0), 0, 8)
        h.send("1f-", (1, 0), 4, 4, (-1, 0))
    for h in halves:
        for q in (-1, 1):
            h.send(f"2+{q}", (q, 0), 0, 8, (0, 1))
            h.send(f"2-{q}", (q, 0), 0, 8, (0, -1))

    def forward(q):
        for h in halves:
            h.recv(f"2+{q}", (q, -1), 0, 8)
            h.send("2f+", (q, -1), 0, 4, (0, 1))
            h.recv(f"2-{q}", (q, 1), 0, 8)
            h.send("2f-", (q, 1), 4, 4, (0, -1))

    forward(0)
    for h in halves:
        h.recv("1f+", (2, 0), 0, 4)
        h.recv("1f-", (2, 0), 4, 4)
        h.send("2+2", (2, 0), 0, 8, (0, 1))
        h.send("2-2", (2, 0), 0, 8, (0, -1))

    own_recv(0, left, 0, TPD)
    own_send(3, left, 0, 8, right)
    own_send(5, left, 0, TPD, sib)
    own_recv(1, right, 0, TPD)
    own_send(4, right, 8, 8, left)
    own_send(6, right, 0, TPD, sib)

    forward(-1)
    forward(1)
    own_recv(3, far, 0, 8)
    own_recv(4, far, 8, 8)
    own_send(7, far, 0, TPD, sib)
    forward(2)
    own_recv(2, sib, 0, TPD)
    for k, c in ((5, left), (6, right), (7, far)):
        own_recv(k, c + 1 - 2 * core, 0, TPD)
    a_copy.wait()
    received(panel.at[pl.ds(0, 64)], ag_s, ag_r.at[0])

    @pl.loop(1, ROWS)
    def _(d):
        remote(metas.at[row], metas.at[row], meta_s, meta_r, at((row + d) & 15, col)).start()

    for dx, dc in XHOPS:
        to = ((x + dx) & 3) * 2 + ((core + dc) & 1)
        remote(slabs.at[col], slabs.at[col], slab_s, slab_r, at(row, to)).start()

    def exchange(chunk, lo, n):
        part = pl.ds(FROM[chunk], PARTS[chunk])
        for dy, dz in HOPS:
            to = ((y + dy) & 3) * 4 + ((z + dz) & 3)
            remote(
                sendbuf.at[to, part, pl.ds(lo, n)], recvbuf.at[part, row, pl.ds(lo, n)],
                ex_s, ex_r.at[chunk], at(to, col),
            ).start()

    def exchange2(chunk, lo, n):
        for dx, dc in XHOPS:
            to = ((x + dx) & 3) * 2 + ((core + dc) & 1)
            remote(
                sendbuf.at[pl.ds(to * 2, 2), pl.ds(SPLIT + FROM2[chunk], PARTS2[chunk]), pl.ds(lo, n)],
                pieces.at[:, pl.ds(FROM2[chunk], PARTS2[chunk]), col, pl.ds(lo, n)],
                pc_s, pc_r.at[chunk], at(row, to),
            ).start()

    @pl.loop(0, GROUPS)
    def _(g):
        lo = pl.multiple_of(g * GT, GT)
        for u in range(GT):
            tile = cols_ref[lo + u]
            prod = jnp.dot(
                a_ref[lo + u, 0], panel[(tile >> 7) * TPD + (tile & 15)], preferred_element_type=F32
            ).astype(BF16)
            terms[u * B:(u + 1) * B, :] = jnp.dot(own[lo + u], prod, preferred_element_type=F32)

        @pl.loop(0, ROWS)
        def _(step):
            for u in range(8):
                sendbuf[step, u, pl.ds(lo, GT), :] = terms[
                    pl.ds(step * 8 + u, GT, stride=B), :
                ].astype(BF16)

        exchange(0, lo, GT)
        exchange2(0, lo, GT)

    for chunk in range(1, CHUNKS2):
        exchange2(chunk, 0, SLAB)
    for chunk in range(1, CHUNKS):
        exchange(chunk, 0, SLAB)
    own_copies = [
        pltpu.make_async_copy(sendbuf.at[row, i], recvbuf.at[i, row], loc_sem.at[1 + i])
        for i in range(SPLIT)
    ] + [
        pltpu.make_async_copy(
            sendbuf.at[col * 2 + h, SPLIT + i], pieces.at[h, i, col], loc_sem.at[1 + SPLIT + h * REST + i]
        )
        for h in range(2) for i in range(REST)
    ]
    for c in own_copies:
        c.start()

    received(metas.at[pl.ds(0, ROWS - 1)], meta_s, meta_r)
    received(slabs.at[pl.ds(0, COLS - 1)], slab_s, slab_r)
    aggs = jnp.concatenate([metas[r, 0:1, :] for r in range(ROWS)], 0).astype(F32).astype(BF16)

    def coarse_column(g):
        lane_hot = jnp.where(iota((SLAB, SLAB), 0) == (g & (SLAB - 1)), 1.0, 0.0).astype(BF16)
        picked = jnp.dot(aggs, lane_hot, preferred_element_type=F32)
        slab_hot = iota((ROWS, SLAB), 0) == (g >> 7)
        return jnp.sum(jnp.where(slab_hot, picked, 0.0), 0, keepdims=True).astype(jnp.int32)

    for c in range(COLS):
        big_j = coarse_column(slabs[c, 1:2, :])
        big_i = slabs[c, 0:1, :]
        dest = (big_i >> 1) * 64 + (big_j >> 2) * 8 + (big_i & 1) * 4 + (big_j & 3)
        for blk in range(COLS):
            hot2[blk * SLAB:(blk + 1) * SLAB, c * SLAB:(c + 1) * SLAB] = jnp.where(
                iota((SLAB, SLAB), 0) + blk * SLAB == dest, 1.0, 0.0
            ).astype(BF16)
    for r in range(ROWS):
        big_j = coarse_column(metas[r, 1:2, :])
        big_i = metas[r, 0:1, :]
        dest = (big_j >> 2) * SLAB + big_i * 4 + (big_j & 3)
        for blk in range(COLS):
            hot[blk * SLAB:(blk + 1) * SLAB, r * SLAB:(r + 1) * SLAB] = jnp.where(
                iota((SLAB, SLAB), 0) + blk * SLAB == dest, 1.0, 0.0
            ).astype(BF16)
    for c in own_copies:
        c.wait()

    def scatter(chunk):
        lo, n = FROM[chunk], PARTS[chunk]
        received(recvbuf.at[pl.ds(lo, n), pl.ds(0, ROWS - 1)], ex_s, ex_r.at[chunk])
        rhs = jnp.concatenate([recvbuf[lo + u].reshape(ROWS * SLAB, B) for u in range(n)], 1)

        @pl.loop(0, COLS)
        def _(blk):
            start = pl.multiple_of(blk * SLAB, SLAB)
            block = jnp.dot(hot[pl.ds(start, SLAB), :], rhs, preferred_element_type=F32)
            for u in range(n):
                xsend[blk, lo + u] = block[:, u * B:(u + 1) * B].astype(BF16)

        for dx, dc in XHOPS:
            to = ((x + dx) & 3) * 2 + ((core + dc) & 1)
            remote(
                xsend.at[to, pl.ds(lo, n)], xrecv.at[pl.ds(lo, n), col],
                cr_s, cr_r.at[chunk], at(row, to),
            ).start()

    def finish(chunk):
        lo, n = FROM[chunk], PARTS[chunk]
        part = pl.ds(lo, n)
        received(xrecv.at[part, pl.ds(0, COLS - 1)], cr_s, cr_r.at[chunk])
        for i in range(lo, lo + n):
            @pl.loop(0, 4)
            def _(q):
                lines = pl.ds(q * 32, 32)
                block = xsend[col, i, lines].astype(F32)
                for d in range(1, COLS):
                    block += xrecv[i, (col + d) & 7, lines].astype(F32)
                total[i, lines] = block

        for dy, dz in HOPS:
            to = ((y + dy) & 3) * 4 + ((z + dz) & 3)
            remote(
                total.at[part, pl.ds(pl.multiple_of(to * 8, 8), 8)], last.at[row, part],
                fin_s, fin_r, at(to, col),
            ).start()
        last[row, part] = total[part, pl.ds(pl.multiple_of(row * 8, 8), 8), :]

    def scatter2(chunk):
        lo, n = FROM2[chunk], PARTS2[chunk]
        part = pl.ds(lo, n)
        received(pieces.at[:, part, pl.ds(0, COLS - 1)], pc_s, pc_r.at[chunk])
        for h in range(2):
            rhs = jnp.concatenate([pieces[h, lo + u].reshape(COLS * SLAB, B) for u in range(n)], 1)

            @pl.loop(0, COLS)
            def _(blk):
                start = pl.multiple_of(blk * SLAB, SLAB)
                block = jnp.dot(hot2[pl.ds(start, SLAB), :], rhs, preferred_element_type=F32)
                for u in range(n):
                    for v in range(2):
                        sums = block[v * 64:(v + 1) * 64, u * B:(u + 1) * B]
                        wide[h, lo + u, blk >> 1, (blk & 1) * 2 + v] = sums
                        dense[h, lo + u, blk >> 1, (blk & 1) * 2 + v] = sums.astype(BF16)

            for d in (1, 3, 2):
                if h == 0:
                    to = (y + d) & 3
                    src, here, dev = dense.at[0, part, to], y, to * 4 + z
                else:
                    to = (z + d) & 3
                    src, here, dev = dense.at[1, part, :, to], z, y * 4 + to
                remote(src, part1.at[h, part, here], p1_s, p1_r.at[chunk, h], at(dev, col)).start()

    def middle2(chunk):
        lo, n = FROM2[chunk], PARTS2[chunk]
        part = pl.ds(lo, n)
        for h in range(2):
            received(part1.at[h, part, pl.ds(0, 3)], p1_s, p1_r.at[chunk, h])
            here = y if h == 0 else z
            for i in range(lo, lo + n):
                for q in range(4):
                    block = wide[0, i, y, q] if h == 0 else wide[1, i, q, z]
                    for d in (1, 2, 3):
                        block += part1[h, i, (here + d) & 3, q].astype(F32)
                    sum1[h, i, q] = block
                    lean[h, i, q] = block.astype(BF16)
            for d in (1, 3, 2):
                if h == 0:
                    to = (z + d) & 3
                    here2, dev = z, y * 4 + to
                else:
                    to = (y + d) & 3
                    here2, dev = y, to * 4 + z
                remote(
                    lean.at[h, part, to], part2.at[h, part, here2], p2_s, p2_r.at[chunk, h], at(dev, col)
                ).start()

    def finish2(chunk):
        lo, n = FROM2[chunk], PARTS2[chunk]
        part = pl.ds(lo, n)
        for h in range(2):
            received(part2.at[h, part, pl.ds(0, 3)], p2_s, p2_r.at[chunk, h])
            here = z if h == 0 else y
            for i in range(lo, lo + n):
                block = sum1[h, i, here]
                for d in (1, 2, 3):
                    block += part2[h, i, (here + d) & 3].astype(F32)
                sum2[h, i] = block.reshape(COLS, 8, B)
        for dx, dc in XHOPS:
            to = ((x + dx) & 3) * 2 + ((core + dc) & 1)
            remote(
                sum2.at[:, part, to], last.at[pl.ds(col * 2, 2), pl.ds(SPLIT + lo, n)],
                p3_s, p3_r, at(row, to),
            ).start()
        for h in range(2):
            for i in range(lo, lo + n):
                last[col * 2 + h, SPLIT + i] = sum2[h, i, col]

    for step in ORDER:
        {"s": scatter, "f": finish, "S": scatter2, "M": middle2, "F": finish2}[step[0]](int(step[1]))
    received(last.at[pl.ds(0, ROWS - 1), pl.ds(0, SPLIT)], fin_s, fin_r)
    received(last.at[pl.ds(0, ROWS - 2), pl.ds(SPLIT, REST)], p3_s, p3_r)

    sent(panel.at[pl.ds(0, 240)], ag_s, ag_r.at[0])
    sent(own.at[pl.ds(0, 112)], x_s, x_r.at[0])
    sent(metas.at[pl.ds(0, ROWS - 1)], meta_s, meta_r)
    sent(slabs.at[pl.ds(0, COLS - 1)], slab_s, slab_r)
    sent(sendbuf.at[pl.ds(0, ROWS - 1), pl.ds(0, SPLIT)], ex_s, ex_r.at[0])
    sent(sendbuf.at[pl.ds(0, ROWS - 2), pl.ds(SPLIT, REST)], pc_s, pc_r.at[0])
    sent(xsend.at[pl.ds(0, COLS - 1)], cr_s, cr_r.at[0])
    sent(last.at[pl.ds(0, ROWS - 1), pl.ds(0, SPLIT)], fin_s, fin_r)
    sent(dense.at[:, :, pl.ds(0, 3)], p1_s, p1_r.at[0, 0])
    sent(lean.at[:, :, pl.ds(0, 3)], p2_s, p2_r.at[0, 0])
    sent(sum2.at[:, :, pl.ds(0, COLS - 1)], p3_s, p3_r)


def shards(a_blocks, p_tiles, owner, agg_local, a_cols):
    vmem = pl.BlockSpec(memory_space=pltpu.VMEM)
    dma = pltpu.SemaphoreType.DMA
    rows = pl.pallas_call(
        kernel,
        out_shape=jax.ShapeDtypeStruct((ROWS, 8, 8, B), F32),
        in_specs=[
            pl.BlockSpec(memory_space=pltpu.SMEM), vmem, vmem, vmem, pl.BlockSpec(memory_space=pl.ANY), pl.BlockSpec(memory_space=pl.ANY)
        ],
        out_specs=vmem,
        scratch_shapes=[
            pltpu.VMEM((SLAB, 1, B, B), BF16),
            pltpu.VMEM((ROWS * TPD, B, B), BF16),
            pltpu.VMEM((COLS * TPD, B, B), BF16),
            pltpu.VMEM((ROWS, 8, SLAB), jnp.int32),
            pltpu.VMEM((COLS, 8, SLAB), jnp.int32),
            pltpu.VMEM((BLOCKS, ROWS * SLAB), BF16),
            pltpu.VMEM((BLOCKS, COLS * SLAB), BF16),
            pltpu.VMEM((GT * B, B), F32),
            pltpu.VMEM((ROWS, 8, SLAB, B), BF16),
            pltpu.VMEM((SPLIT, ROWS, SLAB, B), BF16),
            pltpu.VMEM((COLS, SPLIT, SLAB, B), BF16),
            pltpu.VMEM((SPLIT, COLS, SLAB, B), BF16),
            pltpu.VMEM((SPLIT, SLAB, B), F32),
            pltpu.VMEM((2, REST, COLS, SLAB, B), BF16),
            pltpu.VMEM((2, REST, 4, 4, 64, B), BF16),
            pltpu.VMEM((2, REST, 4, 4, 64, B), F32),
            pltpu.VMEM((2, REST, 4, 4, 64, B), BF16),
            pltpu.VMEM((2, REST, 4, 64, B), F32),
            pltpu.VMEM((2, REST, 4, 64, B), BF16),
            pltpu.VMEM((2, REST, 4, 64, B), BF16),
            pltpu.VMEM((2, REST, COLS, 8, B), F32),
            dma, dma((1 + SPLIT + 2 * REST,)), dma, dma, dma, dma, dma, dma((25,)), dma, dma((8,)),
            dma, dma((CHUNKS,)), dma, dma((CHUNKS,)), dma, dma,
            dma, dma((CHUNKS2,)), dma, dma((CHUNKS2, 2)), dma, dma((CHUNKS2, 2)), dma, dma,
        ],
        compiler_params=pltpu.CompilerParams(
            collective_id=0, has_side_effects=True, vmem_limit_bytes=56 * 1024 * 1024
        ),
    )(
        a_cols.reshape(SLAB), owner.reshape(1, SLAB), agg_local.reshape(1, SLAB),
        a_cols.reshape(1, SLAB), p_tiles, a_blocks,
    )
    return rows.reshape(B, OWN, 4, B).transpose(1, 2, 0, 3)


def solution(mesh):
    in_specs = (
        P("row", "col", None, None),
        P(("row", "col"), None, None),
        P("row", None),
        P("row"),
        P("row", "col"),
    )
    out_specs = P("row", "col", None, None)
    return jax.shard_map(shards, mesh=mesh, in_specs=in_specs, out_specs=out_specs, check_vma=False)
```

```python
import functools

import jax
import jax.numpy as jnp
from jax import lax
from jax.experimental import pallas as pl
from jax.experimental.pallas import tpu as pltpu
from jax.sharding import PartitionSpec as P

MESH = pl.DeviceIdType.MESH
OWN = 2
B = 128
SIDE = 4
ROWS = 16
COLS = 8
TPD = 16
SLAB = 128
NAGG = 32
BLOCKS = NAGG * NAGG
GROUPS = 8
GT = SLAB // GROUPS
PARTS = (2, 2)
PARTS2 = (2, 1, 1)
CHUNKS, CHUNKS2 = len(PARTS), len(PARTS2)
SPLIT = sum(PARTS)
REST = 8 - SPLIT
FROM = tuple(sum(PARTS[:n]) for n in range(CHUNKS))
FROM2 = tuple(sum(PARTS2[:n]) for n in range(CHUNKS2))
HOPS = (
    (1, 0), (3, 0), (0, 1), (0, 3), (1, 1), (3, 3), (1, 3), (3, 1),
    (2, 0), (0, 2), (2, 2), (1, 2), (2, 1), (3, 2), (2, 3),
)
ORDER = ('S0', 's0', 'S1', 'S2', 's1', 'M0', 'M1', 'M2', 'f0', 'F0', 'F1', 'f1', 'F2')
XHOPS = ((1, 0), (3, 0), (1, 1), (3, 1), (2, 0), (2, 1), (0, 1))
F32 = jnp.float32
BF16 = jnp.bfloat16


def iota(shape, dim):
    return lax.broadcasted_iota(jnp.int32, shape, dim)


def kernel(
    cols_ref, owner_ref, local_ref, tiles_ref, p_ref, a_hbm, out_ref,
    a_ref, panel, own, metas, slabs, hot, hot2, terms, sendbuf, recvbuf, xsend, xrecv, total,
    pieces, dense, wide, part1, sum1, lean, part2, sum2,
    a_sem, loc_sem, meta_s, meta_r, slab_s, slab_r, ag_s, ag_r, x_s, x_r, ex_s, ex_r, cr_s, cr_r, fin_s, fin_r,
    pc_s, pc_r, p1_s, p1_r, p2_s, p2_r, p3_s, p3_r,
):
    last = out_ref
    row = lax.axis_index("row")
    col = lax.axis_index("col")
    y, z = row >> 2, row & 3
    x, core = col >> 1, col & 1

    def at(r, c):
        return {"row": r, "col": c}

    def remote(src, dst, ss, rs, dev):
        return pltpu.make_async_remote_copy(
            src_ref=src, dst_ref=dst, send_sem=ss, recv_sem=rs, device_id=dev, device_id_type=MESH
        )

    def received(ref, ss, rs):
        remote(ref, ref, ss, rs, at(row, col)).wait_recv()

    def sent(ref, ss, rs):
        remote(ref, ref, ss, rs, at(row, col)).wait_send()

    right, left = ((x + 1) & 3) * 2 + core, ((x + 3) & 3) * 2 + core
    far = ((x + 2) & 3) * 2 + core
    sib = x * 2 + 1 - core

    barrier = pltpu.get_barrier_semaphore()
    near = [(((y + 1) & 3) * 4 + z, col), (((y + 3) & 3) * 4 + z, col), (y * 4 + ((z + 1) & 3), col),
            (y * 4 + ((z + 3) & 3), col), (row, right), (row, left), (row, sib)]
    for r, c in near:
        pl.semaphore_signal(barrier, inc=1, device_id=at(r, c), device_id_type=MESH)

    a_copy = pltpu.make_async_copy(a_hbm, a_ref, a_sem)
    a_copy.start()
    p_copy = pltpu.make_async_copy(p_ref, panel.at[pl.ds(row * TPD, TPD)], loc_sem.at[0])
    p_copy.start()
    mine = jnp.concatenate(
        [owner_ref[...] * OWN + local_ref[...], tiles_ref[...], jnp.zeros((6, SLAB), jnp.int32)], 0
    )
    metas[row] = mine
    slabs[col] = mine
    pl.semaphore_wait(barrier, len(near))

    class Half:
        sems = {}

        def __init__(self, h):
            self.h = h
            self.f, self.s = (y, z) if h == 0 else (z, y)

        def slot(self, df, ds):
            f, s = (self.f + df) & 3, (self.s + ds) & 3
            return f * SIDE + s if self.h == 0 else s * SIDE + f

        def sem(self, name):
            if name[:2] == "2f":
                return ag_r.at[0]
            return ag_r.at[Half.sems.setdefault((self.h, name), len(Half.sems) + 1)]

        def part(self, slot, lo, n):
            return panel.at[pl.ds(self.slot(*slot) * TPD + 8 * self.h + lo, n)]

        def send(self, name, slot, lo, n, to):
            src = p_ref.at[pl.ds(8 * self.h + lo, n)] if slot == (0, 0) else self.part(slot, lo, n)
            remote(src, self.part(slot, lo, n), ag_s, self.sem(name), at(self.slot(*to), col)).start()

        def recv(self, name, slot, lo, n):
            received(self.part(slot, lo, n), ag_s, self.sem(name))

    halves = [Half(0), Half(1)]
    for h in halves:
        h.send("1+", (0, 0), 0, 8, (1, 0))
        h.send("1-", (0, 0), 0, 8, (-1, 0))
    for h in halves:
        h.send("2+0", (0, 0), 0, 8, (0, 1))
        h.send("2-0", (0, 0), 0, 8, (0, -1))

    p_copy.wait()
    for w in range(TPD):
        own[col * TPD + w] = panel[row * TPD + w].T
    def own_send(k, c, lo, n, to):
        ref = own.at[pl.ds(c * TPD + lo, n)]
        remote(ref, ref, x_s, x_r.at[k], at(row, to)).start()

    def own_recv(k, c, lo, n):
        received(own.at[pl.ds(c * TPD + lo, n)], x_s, x_r.at[k])

    own_send(0, col, 0, TPD, right)
    own_send(1, col, 0, TPD, left)
    own_send(2, col, 0, TPD, sib)

    for h in halves:
        h.recv("1+", (-1, 0), 0, 8)
        h.send("1f+", (-1, 0), 0, 4, (1, 0))
        h.recv("1-", (1, 0), 0, 8)
        h.send("1f-", (1, 0), 4, 4, (-1, 0))
    for h in halves:
        for q in (-1, 1):
            h.send(f"2+{q}", (q, 0), 0, 8, (0, 1))
            h.send(f"2-{q}", (q, 0), 0, 8, (0, -1))

    def forward(q):
        for h in halves:
            h.recv(f"2+{q}", (q, -1), 0, 8)
            h.send("2f+", (q, -1), 0, 4, (0, 1))
            h.recv(f"2-{q}", (q, 1), 0, 8)
            h.send("2f-", (q, 1), 4, 4, (0, -1))

    forward(0)
    for h in halves:
        h.recv("1f+", (2, 0), 0, 4)
        h.recv("1f-", (2, 0), 4, 4)
        h.send("2+2", (2, 0), 0, 8, (0, 1))
        h.send("2-2", (2, 0), 0, 8, (0, -1))

    own_recv(0, left, 0, TPD)
    own_send(3, left, 0, 8, right)
    own_send(5, left, 0, TPD, sib)
    own_recv(1, right, 0, TPD)
    own_send(4, right, 8, 8, left)
    own_send(6, right, 0, TPD, sib)

    forward(-1)
    forward(1)
    own_recv(3, far, 0, 8)
    own_recv(4, far, 8, 8)
    own_send(7, far, 0, TPD, sib)
    forward(2)
    own_recv(2, sib, 0, TPD)
    for k, c in ((5, left), (6, right), (7, far)):
        own_recv(k, c + 1 - 2 * core, 0, TPD)
    a_copy.wait()
    received(panel.at[pl.ds(0, 64)], ag_s, ag_r.at[0])

    @pl.loop(1, ROWS)
    def _(d):
        remote(metas.at[row], metas.at[row], meta_s, meta_r, at((row + d) & 15, col)).start()

    for dx, dc in XHOPS:
        to = ((x + dx) & 3) * 2 + ((core + dc) & 1)
        remote(slabs.at[col], slabs.at[col], slab_s, slab_r, at(row, to)).start()

    def exchange(chunk, lo, n):
        part = pl.ds(FROM[chunk], PARTS[chunk])
        for dy, dz in HOPS:
            to = ((y + dy) & 3) * 4 + ((z + dz) & 3)
            remote(
                sendbuf.at[to, part, pl.ds(lo, n)], recvbuf.at[part, row, pl.ds(lo, n)],
                ex_s, ex_r.at[chunk], at(to, col),
            ).start()

    def exchange2(chunk, lo, n):
        for dx, dc in XHOPS:
            to = ((x + dx) & 3) * 2 + ((core + dc) & 1)
            remote(
                sendbuf.at[pl.ds(to * 2, 2), pl.ds(SPLIT + FROM2[chunk], PARTS2[chunk]), pl.ds(lo, n)],
                pieces.at[:, pl.ds(FROM2[chunk], PARTS2[chunk]), col, pl.ds(lo, n)],
                pc_s, pc_r.at[chunk], at(row, to),
            ).start()

    @pl.loop(0, GROUPS)
    def _(g):
        lo = pl.multiple_of(g * GT, GT)
        for u in range(GT):
            tile = cols_ref[lo + u]
            prod = jnp.dot(
                a_ref[lo + u, 0], panel[(tile >> 7) * TPD + (tile & 15)], preferred_element_type=F32
            ).astype(BF16)
            terms[u * B:(u + 1) * B, :] = jnp.dot(own[lo + u], prod, preferred_element_type=F32)

        @pl.loop(0, ROWS)
        def _(step):
            for u in range(8):
                sendbuf[step, u, pl.ds(lo, GT), :] = terms[
                    pl.ds(step * 8 + u, GT, stride=B), :
                ].astype(BF16)

        exchange(0, lo, GT)
        exchange2(0, lo, GT)

    for chunk in range(1, CHUNKS2):
        exchange2(chunk, 0, SLAB)
    for chunk in range(1, CHUNKS):
        exchange(chunk, 0, SLAB)
    own_copies = [
        pltpu.make_async_copy(sendbuf.at[row, i], recvbuf.at[i, row], loc_sem.at[1 + i])
        for i in range(SPLIT)
    ] + [
        pltpu.make_async_copy(
            sendbuf.at[col * 2 + h, SPLIT + i], pieces.at[h, i, col], loc_sem.at[1 + SPLIT + h * REST + i]
        )
        for h in range(2) for i in range(REST)
    ]
    for c in own_copies:
        c.start()

    received(metas.at[pl.ds(0, ROWS - 1)], meta_s, meta_r)
    received(slabs.at[pl.ds(0, COLS - 1)], slab_s, slab_r)
    aggs = jnp.concatenate([metas[r, 0:1, :] for r in range(ROWS)], 0).astype(F32).astype(BF16)

    def coarse_column(g):
        lane_hot = jnp.where(iota((SLAB, SLAB), 0) == (g & (SLAB - 1)), 1.0, 0.0).astype(BF16)
        picked = jnp.dot(aggs, lane_hot, preferred_element_type=F32)
        slab_hot = iota((ROWS, SLAB), 0) == (g >> 7)
        return jnp.sum(jnp.where(slab_hot, picked, 0.0), 0, keepdims=True).astype(jnp.int32)

    for c in range(COLS):
        big_j = coarse_column(slabs[c, 1:2, :])
        big_i = slabs[c, 0:1, :]
        dest = (big_i >> 1) * 64 + (big_j >> 2) * 8 + (big_i & 1) * 4 + (big_j & 3)
        for blk in range(COLS):
            hot2[blk * SLAB:(blk + 1) * SLAB, c * SLAB:(c + 1) * SLAB] = jnp.where(
                iota((SLAB, SLAB), 0) + blk * SLAB == dest, 1.0, 0.0
            ).astype(BF16)
    for r in range(ROWS):
        big_j = coarse_column(metas[r, 1:2, :])
        big_i = metas[r, 0:1, :]
        dest = (big_j >> 2) * SLAB + big_i * 4 + (big_j & 3)
        for blk in range(COLS):
            hot[blk * SLAB:(blk + 1) * SLAB, r * SLAB:(r + 1) * SLAB] = jnp.where(
                iota((SLAB, SLAB), 0) + blk * SLAB == dest, 1.0, 0.0
            ).astype(BF16)
    for c in own_copies:
        c.wait()

    def scatter(chunk):
        lo, n = FROM[chunk], PARTS[chunk]
        received(recvbuf.at[pl.ds(lo, n), pl.ds(0, ROWS - 1)], ex_s, ex_r.at[chunk])
        rhs = jnp.concatenate([recvbuf[lo + u].reshape(ROWS * SLAB, B) for u in range(n)], 1)

        @pl.loop(0, COLS)
        def _(blk):
            start = pl.multiple_of(blk * SLAB, SLAB)
            block = jnp.dot(hot[pl.ds(start, SLAB), :], rhs, preferred_element_type=F32)
            for u in range(n):
                xsend[blk, lo + u] = block[:, u * B:(u + 1) * B].astype(BF16)

        for dx, dc in XHOPS:
            to = ((x + dx) & 3) * 2 + ((core + dc) & 1)
            remote(
                xsend.at[to, pl.ds(lo, n)], xrecv.at[pl.ds(lo, n), col],
                cr_s, cr_r.at[chunk], at(row, to),
            ).start()

    def finish(chunk):
        lo, n = FROM[chunk], PARTS[chunk]
        part = pl.ds(lo, n)
        received(xrecv.at[part, pl.ds(0, COLS - 1)], cr_s, cr_r.at[chunk])
        for i in range(lo, lo + n):
            @pl.loop(0, 4)
            def _(q):
                lines = pl.ds(q * 32, 32)
                block = xsend[col, i, lines].astype(F32)
                for d in range(1, COLS):
                    block += xrecv[i, (col + d) & 7, lines].astype(F32)
                total[i, lines] = block

        for dy, dz in HOPS:
            to = ((y + dy) & 3) * 4 + ((z + dz) & 3)
            remote(
                total.at[part, pl.ds(pl.multiple_of(to * 8, 8), 8)], last.at[row, part],
                fin_s, fin_r, at(to, col),
            ).start()
        last[row, part] = total[part, pl.ds(pl.multiple_of(row * 8, 8), 8), :]

    def scatter2(chunk):
        lo, n = FROM2[chunk], PARTS2[chunk]
        part = pl.ds(lo, n)
        received(pieces.at[:, part, pl.ds(0, COLS - 1)], pc_s, pc_r.at[chunk])
        for h in range(2):
            rhs = jnp.concatenate([pieces[h, lo + u].reshape(COLS * SLAB, B) for u in range(n)], 1)

            @pl.loop(0, COLS)
            def _(blk):
                start = pl.multiple_of(blk * SLAB, SLAB)
                block = jnp.dot(hot2[pl.ds(start, SLAB), :], rhs, preferred_element_type=F32)
                for u in range(n):
                    for v in range(2):
                        sums = block[v * 64:(v + 1) * 64, u * B:(u + 1) * B]
                        wide[h, lo + u, blk >> 1, (blk & 1) * 2 + v] = sums
                        dense[h, lo + u, blk >> 1, (blk & 1) * 2 + v] = sums.astype(BF16)

            for d in (1, 3, 2):
                if h == 0:
                    to = (y + d) & 3
                    src, here, dev = dense.at[0, part, to], y, to * 4 + z
                else:
                    to = (z + d) & 3
                    src, here, dev = dense.at[1, part, :, to], z, y * 4 + to
                remote(src, part1.at[h, part, here], p1_s, p1_r.at[chunk, h], at(dev, col)).start()

    def middle2(chunk):
        lo, n = FROM2[chunk], PARTS2[chunk]
        part = pl.ds(lo, n)
        for h in range(2):
            received(part1.at[h, part, pl.ds(0, 3)], p1_s, p1_r.at[chunk, h])
            here = y if h == 0 else z
            for i in range(lo, lo + n):
                for q in range(4):
                    block = wide[0, i, y, q] if h == 0 else wide[1, i, q, z]
                    for d in (1, 2, 3):
                        block += part1[h, i, (here + d) & 3, q].astype(F32)
                    sum1[h, i, q] = block
                    lean[h, i, q] = block.astype(BF16)
            for d in (1, 3, 2):
                if h == 0:
                    to = (z + d) & 3
                    here2, dev = z, y * 4 + to
                else:
                    to = (y + d) & 3
                    here2, dev = y, to * 4 + z
                remote(
                    lean.at[h, part, to], part2.at[h, part, here2], p2_s, p2_r.at[chunk, h], at(dev, col)
                ).start()

    def finish2(chunk):
        lo, n = FROM2[chunk], PARTS2[chunk]
        part = pl.ds(lo, n)
        for h in range(2):
            received(part2.at[h, part, pl.ds(0, 3)], p2_s, p2_r.at[chunk, h])
            here = z if h == 0 else y
            for i in range(lo, lo + n):
                block = sum1[h, i, here]
                for d in (1, 2, 3):
                    block += part2[h, i, (here + d) & 3].astype(F32)
                sum2[h, i] = block.reshape(COLS, 8, B)
        for dx, dc in XHOPS:
            to = ((x + dx) & 3) * 2 + ((core + dc) & 1)
            remote(
                sum2.at[:, part, to], last.at[pl.ds(col * 2, 2), pl.ds(SPLIT + lo, n)],
                p3_s, p3_r, at(row, to),
            ).start()
        for h in range(2):
            for i in range(lo, lo + n):
                last[col * 2 + h, SPLIT + i] = sum2[h, i, col]

    for step in ORDER:
        {"s": scatter, "f": finish, "S": scatter2, "M": middle2, "F": finish2}[step[0]](int(step[1]))
    received(last.at[pl.ds(0, ROWS - 1), pl.ds(0, SPLIT)], fin_s, fin_r)
    received(last.at[pl.ds(0, ROWS - 2), pl.ds(SPLIT, REST)], p3_s, p3_r)

    sent(panel.at[pl.ds(0, 240)], ag_s, ag_r.at[0])
    sent(own.at[pl.ds(0, 112)], x_s, x_r.at[0])
    sent(metas.at[pl.ds(0, ROWS - 1)], meta_s, meta_r)
    sent(slabs.at[pl.ds(0, COLS - 1)], slab_s, slab_r)
    sent(sendbuf.at[pl.ds(0, ROWS - 1), pl.ds(0, SPLIT)], ex_s, ex_r.at[0])
    sent(sendbuf.at[pl.ds(0, ROWS - 2), pl.ds(SPLIT, REST)], pc_s, pc_r.at[0])
    sent(xsend.at[pl.ds(0, COLS - 1)], cr_s, cr_r.at[0])
    sent(last.at[pl.ds(0, ROWS - 1), pl.ds(0, SPLIT)], fin_s, fin_r)
    sent(dense.at[:, :, pl.ds(0, 3)], p1_s, p1_r.at[0, 0])
    sent(lean.at[:, :, pl.ds(0, 3)], p2_s, p2_r.at[0, 0])
    sent(sum2.at[:, :, pl.ds(0, COLS - 1)], p3_s, p3_r)


def shards(a_blocks, p_tiles, owner, agg_local, a_cols):
    vmem = pl.BlockSpec(memory_space=pltpu.VMEM)
    dma = pltpu.SemaphoreType.DMA
    rows = pl.pallas_call(
        kernel,
        out_shape=jax.ShapeDtypeStruct((ROWS, 8, 8, B), F32),
        in_specs=[
            pl.BlockSpec(memory_space=pltpu.SMEM), vmem, vmem, vmem, pl.BlockSpec(memory_space=pl.ANY), pl.BlockSpec(memory_space=pl.ANY)
        ],
        out_specs=vmem,
        scratch_shapes=[
            pltpu.VMEM((SLAB, 1, B, B), BF16),
            pltpu.VMEM((ROWS * TPD, B, B), BF16),
            pltpu.VMEM((COLS * TPD, B, B), BF16),
            pltpu.VMEM((ROWS, 8, SLAB), jnp.int32),
            pltpu.VMEM((COLS, 8, SLAB), jnp.int32),
            pltpu.VMEM((BLOCKS, ROWS * SLAB), BF16),
            pltpu.VMEM((BLOCKS, COLS * SLAB), BF16),
            pltpu.VMEM((GT * B, B), F32),
            pltpu.VMEM((ROWS, 8, SLAB, B), BF16),
            pltpu.VMEM((SPLIT, ROWS, SLAB, B), BF16),
            pltpu.VMEM((COLS, SPLIT, SLAB, B), BF16),
            pltpu.VMEM((SPLIT, COLS, SLAB, B), BF16),
            pltpu.VMEM((SPLIT, SLAB, B), F32),
            pltpu.VMEM((2, REST, COLS, SLAB, B), BF16),
            pltpu.VMEM((2, REST, 4, 4, 64, B), BF16),
            pltpu.VMEM((2, REST, 4, 4, 64, B), F32),
            pltpu.VMEM((2, REST, 4, 4, 64, B), BF16),
            pltpu.VMEM((2, REST, 4, 64, B), F32),
            pltpu.VMEM((2, REST, 4, 64, B), BF16),
            pltpu.VMEM((2, REST, 4, 64, B), BF16),
            pltpu.VMEM((2, REST, COLS, 8, B), F32),
            dma, dma((1 + SPLIT + 2 * REST,)), dma, dma, dma, dma, dma, dma((25,)), dma, dma((8,)),
            dma, dma((CHUNKS,)), dma, dma((CHUNKS,)), dma, dma,
            dma, dma((CHUNKS2,)), dma, dma((CHUNKS2, 2)), dma, dma((CHUNKS2, 2)), dma, dma,
        ],
        compiler_params=pltpu.CompilerParams(
            collective_id=0, has_side_effects=True, vmem_limit_bytes=56 * 1024 * 1024
        ),
    )(
        a_cols.reshape(SLAB), owner.reshape(1, SLAB), agg_local.reshape(1, SLAB),
        a_cols.reshape(1, SLAB), p_tiles, a_blocks,
    )
    return rows.reshape(B, OWN, 4, B).transpose(1, 2, 0, 3)


def solution(mesh):
    in_specs = (
        P("row", "col", None, None),
        P(("row", "col"), None, None),
        P("row", None),
        P("row"),
        P("row", "col"),
    )
    out_specs = P("row", "col", None, None)
    return jax.shard_map(shards, mesh=mesh, in_specs=in_specs, out_specs=out_specs, check_vma=False)
```

```python
import functools

import jax
import jax.numpy as jnp
from jax import lax
from jax.experimental import pallas as pl
from jax.experimental.pallas import tpu as pltpu
from jax.sharding import PartitionSpec as P

MESH = pl.DeviceIdType.MESH
OWN = 2
B = 128
SIDE = 4
ROWS = 16
COLS = 8
TPD = 16
SLAB = 128
NAGG = 32
BLOCKS = NAGG * NAGG
GROUPS = 8
GT = SLAB // GROUPS
PARTS = (2, 2)
PARTS2 = (2, 1, 1)
CHUNKS, CHUNKS2 = len(PARTS), len(PARTS2)
SPLIT = sum(PARTS)
REST = 8 - SPLIT
FROM = tuple(sum(PARTS[:n]) for n in range(CHUNKS))
FROM2 = tuple(sum(PARTS2[:n]) for n in range(CHUNKS2))
HOPS = (
    (1, 0), (3, 0), (0, 1), (0, 3), (1, 1), (3, 3), (1, 3), (3, 1),
    (2, 0), (0, 2), (2, 2), (1, 2), (2, 1), (3, 2), (2, 3),
)
ORDER = ('S0', 's0', 'S1', 'S2', 's1', 'M0', 'M1', 'M2', 'f0', 'F0', 'F1', 'f1', 'F2')
XHOPS = ((1, 0), (3, 0), (1, 1), (3, 1), (2, 0), (2, 1), (0, 1))
F32 = jnp.float32
BF16 = jnp.bfloat16


def iota(shape, dim):
    return lax.broadcasted_iota(jnp.int32, shape, dim)


def kernel(
    cols_ref, owner_ref, local_ref, tiles_ref, p_ref, a_hbm, out_ref,
    a_ref, panel, own, metas, slabs, hot, hot2, terms, sendbuf, recvbuf, xsend, xrecv, total,
    pieces, dense, wide, part1, sum1, lean, part2, sum2,
    a_sem, loc_sem, meta_s, meta_r, slab_s, slab_r, ag_s, ag_r, x_s, x_r, ex_s, ex_r, cr_s, cr_r, fin_s, fin_r,
    pc_s, pc_r, p1_s, p1_r, p2_s, p2_r, p3_s, p3_r,
):
    last = out_ref
    row = lax.axis_index("row")
    col = lax.axis_index("col")
    y, z = row >> 2, row & 3
    x, core = col >> 1, col & 1

    def at(r, c):
        return {"row": r, "col": c}

    def remote(src, dst, ss, rs, dev):
        return pltpu.make_async_remote_copy(
            src_ref=src, dst_ref=dst, send_sem=ss, recv_sem=rs, device_id=dev, device_id_type=MESH
        )

    def received(ref, ss, rs):
        remote(ref, ref, ss, rs, at(row, col)).wait_recv()

    def sent(ref, ss, rs):
        remote(ref, ref, ss, rs, at(row, col)).wait_send()

    right, left = ((x + 1) & 3) * 2 + core, ((x + 3) & 3) * 2 + core
    far = ((x + 2) & 3) * 2 + core
    sib = x * 2 + 1 - core

    barrier = pltpu.get_barrier_semaphore()
    near = [(((y + 1) & 3) * 4 + z, col), (((y + 3) & 3) * 4 + z, col), (y * 4 + ((z + 1) & 3), col),
            (y * 4 + ((z + 3) & 3), col), (row, right), (row, left), (row, sib)]
    for r, c in near:
        pl.semaphore_signal(barrier, inc=1, device_id=at(r, c), device_id_type=MESH)

    a_copy = pltpu.make_async_copy(a_hbm, a_ref, a_sem)
    a_copy.start()
    p_copy = pltpu.make_async_copy(p_ref, panel.at[pl.ds(row * TPD, TPD)], loc_sem.at[0])
    p_copy.start()
    mine = jnp.concatenate(
        [owner_ref[...] * OWN + local_ref[...], tiles_ref[...], jnp.zeros((6, SLAB), jnp.int32)], 0
    )
    metas[row] = mine
    slabs[col] = mine
    pl.semaphore_wait(barrier, len(near))

    class Half:
        sems = {}

        def __init__(self, h):
            self.h = h
            self.f, self.s = (y, z) if h == 0 else (z, y)

        def slot(self, df, ds):
            f, s = (self.f + df) & 3, (self.s + ds) & 3
            return f * SIDE + s if self.h == 0 else s * SIDE + f

        def sem(self, name):
            if name[:2] == "2f":
                return ag_r.at[0]
            return ag_r.at[Half.sems.setdefault((self.h, name), len(Half.sems) + 1)]

        def part(self, slot, lo, n):
            return panel.at[pl.ds(self.slot(*slot) * TPD + 8 * self.h + lo, n)]

        def send(self, name, slot, lo, n, to):
            src = p_ref.at[pl.ds(8 * self.h + lo, n)] if slot == (0, 0) else self.part(slot, lo, n)
            remote(src, self.part(slot, lo, n), ag_s, self.sem(name), at(self.slot(*to), col)).start()

        def recv(self, name, slot, lo, n):
            received(self.part(slot, lo, n), ag_s, self.sem(name))

    halves = [Half(0), Half(1)]
    for h in halves:
        h.send("1+", (0, 0), 0, 8, (1, 0))
        h.send("1-", (0, 0), 0, 8, (-1, 0))
    for h in halves:
        h.send("2+0", (0, 0), 0, 8, (0, 1))
        h.send("2-0", (0, 0), 0, 8, (0, -1))

    p_copy.wait()
    for w in range(TPD):
        own[col * TPD + w] = panel[row * TPD + w].T
    def own_send(k, c, lo, n, to):
        ref = own.at[pl.ds(c * TPD + lo, n)]
        remote(ref, ref, x_s, x_r.at[k], at(row, to)).start()

    def own_recv(k, c, lo, n):
        received(own.at[pl.ds(c * TPD + lo, n)], x_s, x_r.at[k])

    own_send(0, col, 0, TPD, right)
    own_send(1, col, 0, TPD, left)
    own_send(2, col, 0, TPD, sib)

    for h in halves:
        h.recv("1+", (-1, 0), 0, 8)
        h.send("1f+", (-1, 0), 0, 4, (1, 0))
        h.recv("1-", (1, 0), 0, 8)
        h.send("1f-", (1, 0), 4, 4, (-1, 0))
    for h in halves:
        for q in (-1, 1):
            h.send(f"2+{q}", (q, 0), 0, 8, (0, 1))
            h.send(f"2-{q}", (q, 0), 0, 8, (0, -1))

    def forward(q):
        for h in halves:
            h.recv(f"2+{q}", (q, -1), 0, 8)
            h.send("2f+", (q, -1), 0, 4, (0, 1))
            h.recv(f"2-{q}", (q, 1), 0, 8)
            h.send("2f-", (q, 1), 4, 4, (0, -1))

    forward(0)
    for h in halves:
        h.recv("1f+", (2, 0), 0, 4)
        h.recv("1f-", (2, 0), 4, 4)
        h.send("2+2", (2, 0), 0, 8, (0, 1))
        h.send("2-2", (2, 0), 0, 8, (0, -1))

    own_recv(0, left, 0, TPD)
    own_send(3, left, 0, 8, right)
    own_send(5, left, 0, TPD, sib)
    own_recv(1, right, 0, TPD)
    own_send(4, right, 8, 8, left)
    own_send(6, right, 0, TPD, sib)

    forward(-1)
    forward(1)
    own_recv(3, far, 0, 8)
    own_recv(4, far, 8, 8)
    own_send(7, far, 0, TPD, sib)
    forward(2)
    own_recv(2, sib, 0, TPD)
    for k, c in ((5, left), (6, right), (7, far)):
        own_recv(k, c + 1 - 2 * core, 0, TPD)
    a_copy.wait()
    received(panel.at[pl.ds(0, 64)], ag_s, ag_r.at[0])

    @pl.loop(1, ROWS)
    def _(d):
        remote(metas.at[row], metas.at[row], meta_s, meta_r, at((row + d) & 15, col)).start()

    for dx, dc in XHOPS:
        to = ((x + dx) & 3) * 2 + ((core + dc) & 1)
        remote(slabs.at[col], slabs.at[col], slab_s, slab_r, at(row, to)).start()

    def exchange(chunk, lo, n):
        part = pl.ds(FROM[chunk], PARTS[chunk])
        for dy, dz in HOPS:
            to = ((y + dy) & 3) * 4 + ((z + dz) & 3)
            remote(
                sendbuf.at[to, part, pl.ds(lo, n)], recvbuf.at[part, row, pl.ds(lo, n)],
                ex_s, ex_r.at[chunk], at(to, col),
            ).start()

    def exchange2(chunk, lo, n):
        for dx, dc in XHOPS:
            to = ((x + dx) & 3) * 2 + ((core + dc) & 1)
            remote(
                sendbuf.at[pl.ds(to * 2, 2), pl.ds(SPLIT + FROM2[chunk], PARTS2[chunk]), pl.ds(lo, n)],
                pieces.at[:, pl.ds(FROM2[chunk], PARTS2[chunk]), col, pl.ds(lo, n)],
                pc_s, pc_r.at[chunk], at(row, to),
            ).start()

    @pl.loop(0, GROUPS)
    def _(g):
        lo = pl.multiple_of(g * GT, GT)
        for u in range(GT):
            tile = cols_ref[lo + u]
            prod = jnp.dot(
                a_ref[lo + u, 0], panel[(tile >> 7) * TPD + (tile & 15)], preferred_element_type=F32
            ).astype(BF16)
            terms[u * B:(u + 1) * B, :] = jnp.dot(own[lo + u], prod, preferred_element_type=F32)

        @pl.loop(0, ROWS)
        def _(step):
            for u in range(8):
                sendbuf[step, u, pl.ds(lo, GT), :] = terms[
                    pl.ds(step * 8 + u, GT, stride=B), :
                ].astype(BF16)

        exchange(0, lo, GT)
        exchange2(0, lo, GT)

    for chunk in range(1, CHUNKS2):
        exchange2(chunk, 0, SLAB)
    for chunk in range(1, CHUNKS):
        exchange(chunk, 0, SLAB)
    own_copies = [
        pltpu.make_async_copy(sendbuf.at[row, i], recvbuf.at[i, row], loc_sem.at[1 + i])
        for i in range(SPLIT)
    ] + [
        pltpu.make_async_copy(
            sendbuf.at[col * 2 + h, SPLIT + i], pieces.at[h, i, col], loc_sem.at[1 + SPLIT + h * REST + i]
        )
        for h in range(2) for i in range(REST)
    ]
    for c in own_copies:
        c.start()

    received(metas.at[pl.ds(0, ROWS - 1)], meta_s, meta_r)
    received(slabs.at[pl.ds(0, COLS - 1)], slab_s, slab_r)
    aggs = jnp.concatenate([metas[r, 0:1, :] for r in range(ROWS)], 0).astype(F32).astype(BF16)

    def coarse_column(g):
        lane_hot = jnp.where(iota((SLAB, SLAB), 0) == (g & (SLAB - 1)), 1.0, 0.0).astype(BF16)
        picked = jnp.dot(aggs, lane_hot, preferred_element_type=F32)
        slab_hot = iota((ROWS, SLAB), 0) == (g >> 7)
        return jnp.sum(jnp.where(slab_hot, picked, 0.0), 0, keepdims=True).astype(jnp.int32)

    for c in range(COLS):
        big_j = coarse_column(slabs[c, 1:2, :])
        big_i = slabs[c, 0:1, :]
        dest = (big_i >> 1) * 64 + (big_j >> 2) * 8 + (big_i & 1) * 4 + (big_j & 3)
        for blk in range(COLS):
            hot2[blk * SLAB:(blk + 1) * SLAB, c * SLAB:(c + 1) * SLAB] = jnp.where(
                iota((SLAB, SLAB), 0) + blk * SLAB == dest, 1.0, 0.0
            ).astype(BF16)
    for r in range(ROWS):
        big_j = coarse_column(metas[r, 1:2, :])
        big_i = metas[r, 0:1, :]
        dest = (big_j >> 2) * SLAB + big_i * 4 + (big_j & 3)
        for blk in range(COLS):
            hot[blk * SLAB:(blk + 1) * SLAB, r * SLAB:(r + 1) * SLAB] = jnp.where(
                iota((SLAB, SLAB), 0) + blk * SLAB == dest, 1.0, 0.0
            ).astype(BF16)
    for c in own_copies:
        c.wait()

    def scatter(chunk):
        lo, n = FROM[chunk], PARTS[chunk]
        received(recvbuf.at[pl.ds(lo, n), pl.ds(0, ROWS - 1)], ex_s, ex_r.at[chunk])
        rhs = jnp.concatenate([recvbuf[lo + u].reshape(ROWS * SLAB, B) for u in range(n)], 1)

        @pl.loop(0, COLS)
        def _(blk):
            start = pl.multiple_of(blk * SLAB, SLAB)
            block = jnp.dot(hot[pl.ds(start, SLAB), :], rhs, preferred_element_type=F32)
            for u in range(n):
                xsend[blk, lo + u] = block[:, u * B:(u + 1) * B].astype(BF16)

        for dx, dc in XHOPS:
            to = ((x + dx) & 3) * 2 + ((core + dc) & 1)
            remote(
                xsend.at[to, pl.ds(lo, n)], xrecv.at[pl.ds(lo, n), col],
                cr_s, cr_r.at[chunk], at(row, to),
            ).start()

    def finish(chunk):
        lo, n = FROM[chunk], PARTS[chunk]
        part = pl.ds(lo, n)
        received(xrecv.at[part, pl.ds(0, COLS - 1)], cr_s, cr_r.at[chunk])
        for i in range(lo, lo + n):
            @pl.loop(0, 4)
            def _(q):
                lines = pl.ds(q * 32, 32)
                block = xsend[col, i, lines].astype(F32)
                for d in range(1, COLS):
                    block += xrecv[i, (col + d) & 7, lines].astype(F32)
                total[i, lines] = block

        for dy, dz in HOPS:
            to = ((y + dy) & 3) * 4 + ((z + dz) & 3)
            remote(
                total.at[part, pl.ds(pl.multiple_of(to * 8, 8), 8)], last.at[row, part],
                fin_s, fin_r, at(to, col),
            ).start()
        last[row, part] = total[part, pl.ds(pl.multiple_of(row * 8, 8), 8), :]

    def scatter2(chunk):
        lo, n = FROM2[chunk], PARTS2[chunk]
        part = pl.ds(lo, n)
        received(pieces.at[:, part, pl.ds(0, COLS - 1)], pc_s, pc_r.at[chunk])
        for h in range(2):
            rhs = jnp.concatenate([pieces[h, lo + u].reshape(COLS * SLAB, B) for u in range(n)], 1)

            @pl.loop(0, COLS)
            def _(blk):
                start = pl.multiple_of(blk * SLAB, SLAB)
                block = jnp.dot(hot2[pl.ds(start, SLAB), :], rhs, preferred_element_type=F32)
                for u in range(n):
                    for v in range(2):
                        sums = block[v * 64:(v + 1) * 64, u * B:(u + 1) * B]
                        wide[h, lo + u, blk >> 1, (blk & 1) * 2 + v] = sums
                        dense[h, lo + u, blk >> 1, (blk & 1) * 2 + v] = sums.astype(BF16)

            for d in (1, 3, 2):
                if h == 0:
                    to = (y + d) & 3
                    src, here, dev = dense.at[0, part, to], y, to * 4 + z
                else:
                    to = (z + d) & 3
                    src, here, dev = dense.at[1, part, :, to], z, y * 4 + to
                remote(src, part1.at[h, part, here], p1_s, p1_r.at[chunk, h], at(dev, col)).start()

    def middle2(chunk):
        lo, n = FROM2[chunk], PARTS2[chunk]
        part = pl.ds(lo, n)
        for h in range(2):
            received(part1.at[h, part, pl.ds(0, 3)], p1_s, p1_r.at[chunk, h])
            here = y if h == 0 else z
            for i in range(lo, lo + n):
                for q in range(4):
                    block = wide[0, i, y, q] if h == 0 else wide[1, i, q, z]
                    for d in (1, 2, 3):
                        block += part1[h, i, (here + d) & 3, q].astype(F32)
                    sum1[h, i, q] = block
                    lean[h, i, q] = block.astype(BF16)
            for d in (1, 3, 2):
                if h == 0:
                    to = (z + d) & 3
                    here2, dev = z, y * 4 + to
                else:
                    to = (y + d) & 3
                    here2, dev = y, to * 4 + z
                remote(
                    lean.at[h, part, to], part2.at[h, part, here2], p2_s, p2_r.at[chunk, h], at(dev, col)
                ).start()

    def finish2(chunk):
        lo, n = FROM2[chunk], PARTS2[chunk]
        part = pl.ds(lo, n)
        for h in range(2):
            received(part2.at[h, part, pl.ds(0, 3)], p2_s, p2_r.at[chunk, h])
            here = z if h == 0 else y
            for i in range(lo, lo + n):
                block = sum1[h, i, here]
                for d in (1, 2, 3):
                    block += part2[h, i, (here + d) & 3].astype(F32)
                sum2[h, i] = block.reshape(COLS, 8, B)
        for dx, dc in XHOPS:
            to = ((x + dx) & 3) * 2 + ((core + dc) & 1)
            remote(
                sum2.at[:, part, to], last.at[pl.ds(col * 2, 2), pl.ds(SPLIT + lo, n)],
                p3_s, p3_r, at(row, to),
            ).start()
        for h in range(2):
            for i in range(lo, lo + n):
                last[col * 2 + h, SPLIT + i] = sum2[h, i, col]

    for step in ORDER:
        {"s": scatter, "f": finish, "S": scatter2, "M": middle2, "F": finish2}[step[0]](int(step[1]))
    received(last.at[pl.ds(0, ROWS - 1), pl.ds(0, SPLIT)], fin_s, fin_r)
    received(last.at[pl.ds(0, ROWS - 2), pl.ds(SPLIT, REST)], p3_s, p3_r)

    sent(panel.at[pl.ds(0, 240)], ag_s, ag_r.at[0])
    sent(own.at[pl.ds(0, 112)], x_s, x_r.at[0])
    sent(metas.at[pl.ds(0, ROWS - 1)], meta_s, meta_r)
    sent(slabs.at[pl.ds(0, COLS - 1)], slab_s, slab_r)
    sent(sendbuf.at[pl.ds(0, ROWS - 1), pl.ds(0, SPLIT)], ex_s, ex_r.at[0])
    sent(sendbuf.at[pl.ds(0, ROWS - 2), pl.ds(SPLIT, REST)], pc_s, pc_r.at[0])
    sent(xsend.at[pl.ds(0, COLS - 1)], cr_s, cr_r.at[0])
    sent(last.at[pl.ds(0, ROWS - 1), pl.ds(0, SPLIT)], fin_s, fin_r)
    sent(dense.at[:, :, pl.ds(0, 3)], p1_s, p1_r.at[0, 0])
    sent(lean.at[:, :, pl.ds(0, 3)], p2_s, p2_r.at[0, 0])
    sent(sum2.at[:, :, pl.ds(0, COLS - 1)], p3_s, p3_r)


def shards(a_blocks, p_tiles, owner, agg_local, a_cols):
    vmem = pl.BlockSpec(memory_space=pltpu.VMEM)
    dma = pltpu.SemaphoreType.DMA
    rows = pl.pallas_call(
        kernel,
        out_shape=jax.ShapeDtypeStruct((ROWS, 8, 8, B), F32),
        in_specs=[
            pl.BlockSpec(memory_space=pltpu.SMEM), vmem, vmem, vmem, pl.BlockSpec(memory_space=pl.ANY), pl.BlockSpec(memory_space=pl.ANY)
        ],
        out_specs=vmem,
        scratch_shapes=[
            pltpu.VMEM((SLAB, 1, B, B), BF16),
            pltpu.VMEM((ROWS * TPD, B, B), BF16),
            pltpu.VMEM((COLS * TPD, B, B), BF16),
            pltpu.VMEM((ROWS, 8, SLAB), jnp.int32),
            pltpu.VMEM((COLS, 8, SLAB), jnp.int32),
            pltpu.VMEM((BLOCKS, ROWS * SLAB), BF16),
            pltpu.VMEM((BLOCKS, COLS * SLAB), BF16),
            pltpu.VMEM(((GT + 1) * B, B), F32),
            pltpu.VMEM((ROWS, 8, SLAB, B), BF16),
            pltpu.VMEM((SPLIT, ROWS, SLAB, B), BF16),
            pltpu.VMEM((COLS, SPLIT, SLAB, B), BF16),
            pltpu.VMEM((SPLIT, COLS, SLAB, B), BF16),
            pltpu.VMEM((SPLIT, SLAB, B), F32),
            pltpu.VMEM((2, REST, COLS, SLAB, B), BF16),
            pltpu.VMEM((2, REST, 4, 4, 64, B), BF16),
            pltpu.VMEM((2, REST, 4, 4, 64, B), F32),
            pltpu.VMEM((2, REST, 4, 4, 64, B), BF16),
            pltpu.VMEM((2, REST, 4, 64, B), F32),
            pltpu.VMEM((2, REST, 4, 64, B), BF16),
            pltpu.VMEM((2, REST, 4, 64, B), BF16),
            pltpu.VMEM((2, REST, COLS, 8, B), F32),
            dma, dma((1 + SPLIT + 2 * REST,)), dma, dma, dma, dma, dma, dma((25,)), dma, dma((8,)),
            dma, dma((CHUNKS,)), dma, dma((CHUNKS,)), dma, dma,
            dma, dma((CHUNKS2,)), dma, dma((CHUNKS2, 2)), dma, dma((CHUNKS2, 2)), dma, dma,
        ],
        compiler_params=pltpu.CompilerParams(
            collective_id=0, has_side_effects=True, vmem_limit_bytes=56 * 1024 * 1024
        ),
    )(
        a_cols.reshape(SLAB), owner.reshape(1, SLAB), agg_local.reshape(1, SLAB),
        a_cols.reshape(1, SLAB), p_tiles, a_blocks,
    )
    return rows.reshape(B, OWN, 4, B).transpose(1, 2, 0, 3)


def solution(mesh):
    in_specs = (
        P("row", "col", None, None),
        P(("row", "col"), None, None),
        P("row", None),
        P("row"),
        P("row", "col"),
    )
    out_specs = P("row", "col", None, None)
    return jax.shard_map(shards, mesh=mesh, in_specs=in_specs, out_specs=out_specs, check_vma=False)
```
